32 devices in a mesh: seq: 4 (over z), head: 8 (over y, x, core).
Axes of the slice: x: 2, y: 2, z: 4, core: 2. Of those that a mesh axis runs over, the one named last changes fastest.
Arguments:
- query: bfloat16 [40, 512, 128], P('head', 'seq'), may hold values from -1024 to 1024
- key: bfloat16 [40, 512, 128], P('head', 'seq'), may hold values from -1024 to 1024
- value: bfloat16 [40, 512, 128], P('head', 'seq'), may hold values from -6 to 6
- q_gain: float32 [40, 128], replicated, may hold values from 0.8 to 2
- k_gain: float32 [40, 128], replicated, may hold values from 0.8 to 2
- order: int32 [40, 512], P('head', 'seq'), may hold values from 0 to 511, as said below
- cluster_rows: int32 [40, 4], P('head'), may hold values from 0 to 256, as said below
- block_map: int32 [40, 8, 8], P('head'), may hold values 0 or 1
Outputs:
- attended: bfloat16 [40, 512, 128], P('head', 'seq')
The draws below stay inside these ranges and needn't reach their ends.
Inputs may be any that keep to these rules, and one draw needn't show every extreme that they name: `order`: each stream's row lists every token row once: the rows of cluster 0 first, then those of cluster 1, and so on, in the counts of cluster_rows. `cluster_rows`: each stream's counts sum to 512; of the 128 token rows of one seq index at most 64 belong to one cluster, and in every stream one cluster takes exactly 64 rows from every seq index.
All inputs are finite; a program needn't handle non-finite values. No bound on the sum of `block_map` on one device may be relied on, other than what follows from the above.
Results may differ from the reference program's by a relative error of at most 0.012.
The reference program's roundings to bfloat16 on the way count: a program that leaves them out, or rounds other values in their place, can miss the bound.
Values may be sent and summed in bfloat16 or wider, within the bound.
No kernel may reach another device: no remote copies, remote signals or barrier semaphores. Data moves between devices by JAX's collectives and lax.ppermute only.
A program may use at most 64 MiB of HBM per device.

```python
import math
import jax
import jax.numpy as jnp
from jax import lax

H = 40
DH = 128
TOK_DEV = 128
BLOCK = 128
VIDEOS = 1
STREAMS = 40
LENGTH = 512
CLUSTERS = 4
SLOT = 64
CAP = 256
NBALL = 8


def routing(key):
    base_key = jax.random.fold_in(key, 7001)
    key_heavy, key_pair, key_move, key_shuffle, key_rank = jax.random.split(base_key, 5)
    owners = CLUSTERS
    others = owners - 1
    heavy = jax.random.randint(key_heavy, (STREAMS,), 0, owners)
    rest_rows = TOK_DEV - SLOT
    other_slot = jnp.arange(others, dtype=jnp.int32)
    even_count = rest_rows // others + (other_slot < rest_rows % others).astype(jnp.int32)
    pair_noise = jax.random.randint(key_pair, (STREAMS, owners, others), 0, 2 ** 20) * others + other_slot
    pair_order = jnp.argsort(pair_noise, axis=-1).astype(jnp.int32)
    placed = even_count[pair_order]
    pair_count = others // 2
    if pair_count > 0:
        lead_count = placed[..., 0:2 * pair_count:2]
        follow_count = placed[..., 1:2 * pair_count:2]
        lowest = -jnp.minimum(follow_count, SLOT - lead_count)
        highest = jnp.minimum(lead_count, SLOT - follow_count)
        moved = jax.random.randint(key_move, lead_count.shape, lowest, highest + 1)
        paired = jnp.stack([lead_count - moved, follow_count + moved], axis=-1)
        paired = paired.reshape(STREAMS, owners, 2 * pair_count)
        placed = jnp.concatenate([paired, placed[..., 2 * pair_count:]], axis=-1)
    undo_order = jnp.argsort(pair_order, axis=-1)
    counts_other = jnp.take_along_axis(placed, undo_order, axis=-1)
    other_owner = other_slot[None, :] + (other_slot[None, :] >= heavy[:, None]).astype(jnp.int32)
    owner_axis = jnp.arange(owners, dtype=jnp.int32)
    spread_hit = (other_owner[:, :, None] == owner_axis).astype(jnp.int32)
    route_count = jnp.sum(counts_other[:, :, :, None] * spread_hit[:, None, :, :], axis=2)
    route_count = route_count + SLOT * (heavy[:, None, None] == owner_axis).astype(jnp.int32)
    route_bound = jnp.cumsum(route_count, axis=-1)
    token_slot = jnp.arange(TOK_DEV, dtype=jnp.int32)
    owner_label = jnp.sum((route_bound[:, :, None, :] <= token_slot[None, None, :, None]).astype(jnp.int32), axis=-1)
    shuffle_score = jax.random.randint(key_shuffle, (STREAMS, owners, TOK_DEV), 0, 2 ** 20) * TOK_DEV + token_slot
    owner_label = jnp.take_along_axis(owner_label, jnp.argsort(shuffle_score, axis=-1), axis=-1)
    owner_label = owner_label.reshape(STREAMS, LENGTH)
    token_ids = jnp.arange(LENGTH, dtype=jnp.int32)
    token_rank = jnp.argsort(jax.random.randint(key_rank, (STREAMS, LENGTH), 0, 2 ** 17) * LENGTH + token_ids, axis=-1)
    order_out = jnp.argsort(owner_label * LENGTH + token_rank.astype(jnp.int32), axis=-1).astype(jnp.int32)
    cluster_size = jnp.sum(route_count, axis=1).astype(jnp.int32)
    return (order_out, cluster_size)


def scaled(key, salt, rise_ratio):
    key_base, key_channel, key_token = jax.random.split(jax.random.fold_in(key, salt), 3)
    head_ids = (jnp.arange(STREAMS) % H).astype(jnp.float32)
    rise = rise_ratio ** (head_ids / (H - 1))
    channel_scale = jnp.exp(jax.random.uniform(key_channel, (STREAMS, 1, DH), minval=math.log(0.5), maxval=math.log(2.0)))
    token_scale = jnp.exp(jax.random.uniform(key_token, (VIDEOS, 1, LENGTH, 1), minval=0.0, maxval=math.log(10.0)))
    token_scale = jnp.broadcast_to(token_scale, (VIDEOS, H, LENGTH, 1)).reshape(STREAMS, LENGTH, 1)
    drawn = jax.random.normal(key_base, (STREAMS, LENGTH, DH), dtype=jnp.float32)
    return drawn * rise[:, None, None] * channel_scale * token_scale


def draw_order(key, part):
    return routing(key)[0]


def draw_cluster_rows(key, part):
    return routing(key)[1]


def draw_query(key, part):
    drawn = scaled(key, 7301, 1.94)
    return jnp.clip(drawn, -1024.0, 1024.0).astype(jnp.bfloat16)


def draw_key(key, part):
    drawn = scaled(key, 7302, 1.94)
    return jnp.clip(drawn, -1024.0, 1024.0).astype(jnp.bfloat16)


def touch_ends(result, rng, least, high):
    index_at = [jax.random.randint(jax.random.fold_in(rng, axis), (), 0, length) for axis, length in enumerate(result.shape)]
    longest = result.shape.index(max(result.shape))
    beside = index_at[:longest] + [(index_at[longest] + 1) % result.shape[longest]] + index_at[longest + 1:]
    return result.at[tuple(index_at)].set(least).at[tuple(beside)].set(high)


def block_scale(stream_key, dims, cuts, least, high):
    def one(dim, shards_of):
        draws = jax.random.uniform(jax.random.fold_in(jax.random.fold_in(stream_key, 6), dim), (shards_of,), jnp.float32, least / len(cuts), high / len(cuts))
        return jnp.repeat(jnp.exp(draws), dims[dim] // shards_of).reshape((-1,) + (1,) * (len(dims) - dim - 1))

    level = one(*cuts[0])
    for cut in cuts[1:]:
        level = level * one(*cut)
    return level


def bell_draw(key, shape, width, bound, cuts=(), kind=jnp.bfloat16):
    values = width * jax.random.normal(key, shape, jnp.float32)
    if cuts:
        values = values * block_scale(key, shape, cuts, -0.22, 0.18)
    return jnp.clip(values, -bound, bound).astype(kind)


def setup_inputs(seed: int = 0) -> dict:
    splits = jax.random.split(jax.random.key(seed), 9)
    query = draw_query(jax.random.fold_in(splits[8], 71), 0)
    key = draw_key(jax.random.fold_in(splits[8], 71), 0)
    value = bell_draw(splits[2], (STREAMS, LENGTH, DH), 1.0, 6.0, ((0, 8), (1, 4)))
    q_gain = jnp.clip(jnp.exp(jax.random.uniform(splits[3], (H, DH), jnp.float32, math.log(0.8), math.log(2.0))), 0.8, 2.0)
    k_gain = jnp.clip(jnp.exp(jax.random.uniform(splits[4], (H, DH), jnp.float32, math.log(0.8), math.log(2.0))), 0.8, 2.0)
    order = draw_order(jax.random.fold_in(splits[8], 71), 0)
    cluster_rows = draw_cluster_rows(jax.random.fold_in(splits[8], 71), 0)
    block_map = touch_ends((jax.random.randint(splits[7], (STREAMS, NBALL, NBALL), 0, 2) < 1).astype(jnp.int32), jax.random.fold_in(splits[7], 1), 0, 1)
    return {"query": query, "key": key, "value": value, "q_gain": q_gain, "k_gain": k_gain, "order": order, "cluster_rows": cluster_rows, "block_map": block_map}


epsilon = 1e-06

def reference(query, key, value, q_gain, k_gain, order, cluster_rows, block_map):
    streams, seq_length, head_width = query.shape
    head_count = q_gain.shape[0]
    videos = streams // head_count

    def normalize(rows, gain):
        widened = rows.astype(jnp.float32).reshape(videos, head_count, seq_length, head_width)
        mean_square = lax.optimization_barrier(jnp.mean(jnp.square(widened), axis=(1, 3), keepdims=True))
        normed = widened * lax.rsqrt(mean_square + epsilon) * gain[None, :, None, :]
        return normed.reshape(streams, seq_length, head_width).astype(jnp.bfloat16)
    normed_q = normalize(query, q_gain)
    normed_k = normalize(key, k_gain)
    blocks_per = CAP // BLOCK
    score_scale = head_width ** (-0.5)

    def one_stream(inputs):
        stream_q, stream_k, stream_v, stream_order, stream_rows, stream_map = inputs
        positions = jnp.arange(seq_length, dtype=jnp.int32)
        inverse = jnp.zeros((seq_length,), jnp.int32).at[stream_order].set(positions)
        starts = jnp.cumsum(stream_rows, dtype=jnp.int32) - stream_rows
        owner_id = lax.optimization_barrier(jnp.sum((starts[None, :] <= inverse[:, None]).astype(jnp.int32), axis=1, dtype=jnp.int32)) - 1
        within_row = inverse - starts[owner_id]
        block_id = owner_id * blocks_per + within_row // BLOCK
        allowed = (stream_map[block_id][:, block_id] == 1) | (block_id[:, None] == block_id[None, :])
        scores = jnp.dot(stream_q, stream_k.T, preferred_element_type=jnp.float32) * score_scale
        masked = jnp.where(allowed, scores, -jnp.inf)
        row_peak = lax.optimization_barrier(jnp.max(masked, axis=1, keepdims=True))
        probs = jnp.where(allowed, jnp.exp(masked - row_peak), 0.0)
        denom_sum = lax.optimization_barrier(jnp.sum(probs, axis=1, keepdims=True))
        mixed = jnp.dot(probs.astype(jnp.bfloat16), stream_v, preferred_element_type=jnp.float32) / denom_sum
        return mixed.astype(jnp.bfloat16)
    return lax.map(one_stream, (normed_q, normed_k, value, order, cluster_rows, block_map))
```

```python
import functools
import math

import jax
import jax.numpy as jnp
from jax import lax
from jax.experimental import pallas as pl
from jax.experimental.pallas import tpu as pltpu
from jax.sharding import PartitionSpec as P

BLOCK = 128
LANES = 128
epsilon = 1e-06
far = -1e30

NT = (((1,), (1,)), ((), ()))
NN = (((1,), (0,)), ((), ()))
VMEM = pl.BlockSpec(memory_space=pltpu.VMEM)
SMEM = pl.BlockSpec(memory_space=pltpu.SMEM)


def dot(a, b, dims, precision=None):
    return lax.dot_general(a, b, dims, precision=precision, preferred_element_type=jnp.float32)


def sums_kernel(streams, query, key, order, sums, order_rows):
    rows = sums.shape[0]
    ones = jnp.ones((8, query.shape[2]), jnp.float32)
    totals = []
    for ref in (query, key):
        total = None
        for s in range(streams):
            wide = ref[s].astype(jnp.float32)
            total = wide * wide if total is None else total + wide * wide
        totals.append(dot(ones, total, NT, lax.Precision.HIGHEST))
    row = lax.broadcasted_iota(jnp.int32, totals[0].shape, 0)
    sums[...] = jnp.zeros_like(sums)
    order_rows[...] = jnp.zeros_like(order_rows)
    sums[0:8, :] = jnp.where(row == 0, totals[0], jnp.where(row == 1, totals[1], 0.0))
    order_rows[2 : 2 + streams, :] = order[...].astype(jnp.float32)


def attend_kernel(plan, place, *refs):
    n, streams, half, heads, tok, width = plan
    notes, refs = refs[:n], refs[n:]
    query, key, value, q_gain, k_gain, bounds, table = refs[:7]
    messages = refs[7 : 7 + n - 1]
    out_own, out_peer = refs[7 + n - 1 :]
    rest = streams - 2 * half
    my_seq, first_head = place[0], place[1]
    parity = lax.rem(my_seq, 2)
    norm_width = heads * width
    factor = width ** (-0.5) * math.log2(math.e)
    columns = [notes[m][...].T for m in range(n)]

    def scale(m, row):
        return lax.rsqrt(columns[m][:, row : row + 1] / norm_width + epsilon)

    scale_k = [scale(m, 1) for m in range(n)]
    scale_q = [scale(m, 0) for m in range(2)]
    base = [lax.bitwise_xor(my_seq, m) * tok for m in range(n)]
    lane_pos = lax.broadcasted_iota(jnp.int32, (tok, tok), 0)
    tokens = [(lane_pos + base[m]).astype(jnp.float32) for m in range(n)]

    def normal(rows, scales, gain):
        return (rows.astype(jnp.float32) * scales * gain).astype(jnp.bfloat16)

    def attend(s, q_rows, k_rows, v_rows):
        gain_q = q_gain[pl.ds(first_head + s, 1), :]
        gain_k = k_gain[pl.ds(first_head + s, 1), :]
        count = len(q_rows)
        low = bounds[pl.ds(2 * s, 1), :]
        high = bounds[pl.ds(2 * s + 1, 1), :]
        blocks = []
        for m in range(n):
            wide = jnp.concatenate([tokens[m]] * (bounds.shape[1] // tok), axis=1)
            blocks.append(((low <= wide) & (wide < high)).astype(jnp.float32).astype(jnp.bfloat16))
        place_block = jnp.concatenate(blocks, axis=0)
        hits = []
        for m in range(n):
            row = []
            for j in range(n):
                ids = notes[j][pl.ds(2 + s, 1), :]
                row.append((tokens[m] == ids).astype(jnp.float32).astype(jnp.bfloat16))
            hits.append(jnp.concatenate(row, axis=1))
        hit = jnp.concatenate(hits, axis=0)
        member = dot(hit, place_block, NN).astype(jnp.bfloat16)
        bias = dot(member[: count * tok], table[s], NN).astype(jnp.bfloat16)
        normed_q = jnp.concatenate([normal(q_rows[m], scale_q[m], gain_q) for m in range(count)], axis=0)
        normed_k = jnp.concatenate([normal(k_rows[m], scale_k[m], gain_k) for m in range(n)], axis=0)
        scores = dot(
            jnp.concatenate([normed_q, bias], axis=1), jnp.concatenate([normed_k, member], axis=1), NT
        )
        peak = jnp.max(scores, axis=1, keepdims=True)
        weights = jnp.exp2((scores - peak) * factor)
        denom = jnp.sum(weights, axis=1, keepdims=True)
        mixed = dot(weights.astype(jnp.bfloat16), jnp.concatenate(v_rows, axis=0), NN)
        return (mixed / denom).astype(jnp.bfloat16)

    for i in range(half):
        s = parity * half + i
        q_rows = [query[s], messages[0][2 * (half + rest) + i]]
        k_rows = [key[s]] + [messages[m - 1][i] for m in range(1, n)]
        v_rows = [value[s]] + [messages[m - 1][half + rest + i] for m in range(1, n)]
        out = attend(s, q_rows, k_rows, v_rows)
        out_own[i] = out[:tok]
        out_peer[i] = out[tok:]
    for i in range(rest):
        s = 2 * half + i
        k_rows = [key[s]] + [messages[m - 1][half + i] for m in range(1, n)]
        v_rows = [value[s]] + [messages[m - 1][half + rest + half + i] for m in range(1, n)]
        out_own[half + i] = attend(s, [query[s]], k_rows, v_rows)


def local(n, query, key, value, q_gain, k_gain, order, cluster_rows, block_map):
    streams, tok, width = query.shape
    heads = q_gain.shape[0]
    seq_rank = lax.axis_index("seq")
    head_rank = lax.axis_index("head")
    half = streams // 2
    rest = streams - 2 * half
    block_count = block_map.shape[2]
    clusters = cluster_rows.shape[1]
    blocks_per = block_count // clusters
    padded = -(-block_count // LANES) * LANES
    parity = seq_rank % 2

    def exchange(rows, m):
        return lax.ppermute(rows, "seq", [(i, i ^ m) for i in range(n)])

    def parcel(rows, member):
        return [lax.dynamic_slice_in_dim(rows, member * half, half, 0), rows[2 * half :]]

    messages = {}
    for m in reversed(range(1, n)):
        member = parity ^ (m & 1)
        parts = parcel(key, member) + parcel(value, member)
        if m == 1:
            parts += parcel(query, member)[:1]
        messages[m] = exchange(jnp.concatenate(parts, axis=0), m)

    note_rows = -(-(streams + 2) // 8) * 8
    sums, order_rows = pl.pallas_call(
        functools.partial(sums_kernel, streams),
        out_shape=[jax.ShapeDtypeStruct((note_rows, tok), jnp.float32)] * 2,
        in_specs=[VMEM] * 3,
        out_specs=[VMEM] * 2,
    )(query, key, order)
    head_size = lax.axis_size("head")
    step = 1
    while step * streams < heads:
        sums = sums + lax.ppermute(sums, "head", [(i, i ^ step) for i in range(head_size)])
        step *= 2
    note = sums + order_rows
    notes = [note] + [None] * (n - 1)
    for m in reversed(range(1, n)):
        notes[m] = exchange(note, m)

    start = jnp.cumsum(cluster_rows, axis=1, dtype=jnp.int32) - cluster_rows
    step_rows = jnp.arange(blocks_per, dtype=jnp.int32) * BLOCK
    low = start[:, :, None] + step_rows
    high = jnp.minimum(low + BLOCK, (start + cluster_rows)[:, :, None])
    bounds = jnp.stack([low.reshape(streams, block_count), high.reshape(streams, block_count)], axis=1)
    bounds = jnp.pad(
        bounds.reshape(2 * streams, block_count).astype(jnp.float32), ((0, 0), (0, padded - block_count))
    )
    allowed = (block_map == 1) | jnp.eye(block_count, dtype=bool)
    pad = (0, padded - block_count)
    table = jnp.pad(jnp.where(allowed, 0.0, far).astype(jnp.bfloat16), ((0, 0), pad, pad))

    place = jnp.stack([seq_rank, (head_rank * streams) % heads]).astype(jnp.int32)
    own, peer = pl.pallas_call(
        functools.partial(attend_kernel, (n, streams, half, heads, tok, width)),
        out_shape=[
            jax.ShapeDtypeStruct((half + rest, tok, width), jnp.bfloat16),
            jax.ShapeDtypeStruct((half, tok, width), jnp.bfloat16),
        ],
        in_specs=[SMEM] + [VMEM] * (n + 7 + n - 1),
        out_specs=[VMEM] * 2,
        compiler_params=pltpu.CompilerParams(vmem_limit_bytes=48 * 1024 * 1024),
    )(place, *notes, query, key, value, q_gain, k_gain, bounds, table, *[messages[m] for m in range(1, n)])
    theirs = exchange(peer, 1)
    first = jnp.where(parity == 0, own[:half], theirs)
    second = jnp.where(parity == 0, theirs, own[:half])
    return jnp.concatenate([first, second, own[half:]], axis=0)


def solution(mesh):
    return jax.shard_map(
        functools.partial(local, mesh.shape["seq"]),
        mesh=mesh,
        in_specs=(
            P("head", "seq", None),
            P("head", "seq", None),
            P("head", "seq", None),
            P(),
            P(),
            P("head", "seq"),
            P("head", None),
            P("head", None, None),
        ),
        out_specs=P("head", "seq", None),
        check_vma=False,
    )
```

```python
import functools
import math

import jax
import jax.numpy as jnp
from jax import lax
from jax.experimental import pallas as pl
from jax.experimental.pallas import tpu as pltpu
from jax.sharding import PartitionSpec as P

BLOCK = 128
LANES = 128
epsilon = 1e-06
far = -1e30
weight = 20_000_000_000

NT = (((1,), (1,)), ((), ()))
NN = (((1,), (0,)), ((), ()))
VMEM = pl.BlockSpec(memory_space=pltpu.VMEM)
ANY = pl.BlockSpec(memory_space=pl.ANY)
limit = pltpu.CompilerParams(vmem_limit_bytes=48 * 1024 * 1024)


def dot(a, b, dims, precision=None):
    return lax.dot_general(a, b, dims, precision=precision, preferred_element_type=jnp.float32)


def one_hot(hit):
    return hit.astype(jnp.float32).astype(jnp.bfloat16)


def call(body, shapes, args, cost=None, **more):
    return pl.pallas_call(
        body,
        out_shape=shapes,
        in_specs=[VMEM] * len(args),
        out_specs=jax.tree.map(lambda _: VMEM, shapes),
        compiler_params=limit,
        cost_estimate=cost and pl.CostEstimate(flops=cost, bytes_accessed=0, transcendentals=0),
        **more,
    )(*args)


def prep_kernel(half, tail, query, key, value, order, note, same, other, plain, q_in, k_in, order_in, sems):
    streams, tok, width = query.shape
    rest = streams - 2 * half
    parity = lax.rem(lax.axis_index("seq"), 2)
    pairs = [(query, q_in), (key, k_in), (order, order_in)]
    for target, side in ((plain, 1 - parity), (same, parity), (other, 1 - parity)):
        for i in range(half):
            pairs.append((value.at[side * half + i], target.at[pl.ds(i * tok, tok)]))
        if target is plain:
            continue
        for i, s in enumerate(range(2 * half, streams)):
            for j, ref in enumerate((value, key)):
                pairs.append((ref.at[s], target.at[pl.ds((half + 2 * i + j) * tok, tok)]))
        if target is other:
            for i in range(half):
                pairs.append((query.at[side * half + i], target.at[pl.ds((half + 2 * rest + i) * tok, tok)]))
    copies = [pltpu.make_async_copy(src, dst, sems.at[i]) for i, (src, dst) in enumerate(pairs)]
    for copy in copies:
        copy.start()
    ones = jnp.ones((8, width), jnp.float32)
    totals = []
    for copy, ref in zip(copies, (q_in, k_in)):
        copy.wait()
        total = None
        for s in range(streams):
            wide = ref[s].astype(jnp.float32)
            total = wide * wide if total is None else total + wide * wide
        totals.append(dot(ones, total, NT, lax.Precision.HIGHEST))
    row = lax.broadcasted_iota(jnp.int32, totals[0].shape, 0)
    note[...] = jnp.where(row == 0, totals[0], jnp.where(row == 1, totals[1], 0.0))
    copies[2].wait()
    row = lax.broadcasted_iota(jnp.int32, (tail, tok), 0)
    for side, targets in ((1 - parity, (plain, other)), (parity, (same,))):
        rows = jnp.zeros((tail, tok), jnp.float32)
        for i in range(streams - half):
            s = side * half + i if i < half else half + i
            ids = order_in[pl.ds(s, 1), :].astype(jnp.float32)
            high = jnp.floor(ids / tok)
            rows = jnp.where(row == 2 * i, high, jnp.where(row == 2 * i + 1, ids - high * tok, rows))
        for target in targets:
            target[target.shape[0] - tail :, :] = rows.astype(jnp.bfloat16)
    for copy in copies[3:]:
        copy.wait()


def norm_kernel(half, heads, totals, query, key, q_gain, k_gain, same, other, own):
    streams, tok, width = query.shape
    kept = streams - half
    parity = lax.rem(lax.axis_index("seq"), 2)
    first_head = lax.rem(lax.axis_index("head") * streams, heads)
    scales = lax.rsqrt(totals[...] / (heads * width) + epsilon)
    columns = scales.T

    def normal(ref, gains, s, column):
        gain = gains[pl.ds(first_head + s, 1), :]
        return (ref[s].astype(jnp.float32) * columns[:, column : column + 1] * gain).astype(jnp.bfloat16)

    row = lax.broadcasted_iota(jnp.int32, (16, tok), 0)
    rows = jnp.zeros((16, tok), jnp.float32)
    for j in range(2):
        piece = scales[j : j + 1, :]
        for i in range(3):
            cut = piece.astype(jnp.bfloat16).astype(jnp.float32)
            rows = jnp.where(row == 3 * j + i, cut, rows)
            piece = piece - cut
    rows = rows.astype(jnp.bfloat16)
    for target in (same, other):
        target[target.shape[0] - 16 :, :] = rows
    for i in range(half):
        mine, theirs = parity * half + i, (1 - parity) * half + i
        at = pl.ds(i * tok, tok)
        same[at, :] = normal(key, k_gain, mine, 1)
        other[at, :] = normal(key, k_gain, theirs, 1)
        own[at, :] = normal(query, q_gain, mine, 0)
    for s in range(2 * half, streams):
        own[pl.ds((s - half) * tok, tok), :] = normal(query, q_gain, s, 0)
        own[pl.ds((kept + s - 2 * half) * tok, tok), :] = normal(key, k_gain, s, 1)


def table_kernel(half, i, block_map, table):
    count = block_map.shape[1]
    s = lax.rem(lax.axis_index("seq"), 2) * half + i if i < half else half + i
    row = lax.broadcasted_iota(jnp.int32, (count, count), 0)
    column = lax.broadcasted_iota(jnp.int32, (count, count), 1)
    table[...] = jnp.zeros_like(table)
    table[:count, :count] = jnp.where((block_map[s] == 1) | (row == column), 0.0, far)


def blocks_kernel(half, i, bounds, table, *refs):
    notes, member, bias_out = refs[:-2], refs[-2], refs[-1]
    n = len(notes)
    tok = notes[0].shape[1]
    padded = bounds.shape[1]
    tail = notes[0].shape[0] % tok
    my_seq = lax.axis_index("seq")
    s = lax.rem(my_seq, 2) * half + i if i < half else half + i
    row_in = lax.broadcasted_iota(jnp.int32, (tok, LANES), 0)
    tokens = [(row_in + lax.bitwise_xor(my_seq, m) * tok).astype(jnp.float32) for m in range(n)]
    low = bounds[pl.ds(2 * s, 1), :]
    high = bounds[pl.ds(2 * s + 1, 1), :]
    blocks = []
    ids = []
    for m in range(n):
        wide = jnp.concatenate([tokens[m]] * (padded // LANES), axis=1)
        blocks.append(one_hot((low <= wide) & (wide < high)))
        rows = notes[m][notes[m].shape[0] - tail :, :].astype(jnp.float32)
        ids.append(rows[2 * i : 2 * i + 1, :] * tok + rows[2 * i + 1 : 2 * i + 2, :])
    place_block = jnp.concatenate(blocks, axis=0)
    hit = jnp.concatenate(
        [jnp.concatenate([one_hot(tokens[m] == ids[j]) for j in range(n)], axis=1) for m in range(n)], axis=0
    )
    found = dot(hit, place_block, NN).astype(jnp.bfloat16)
    member[...] = found
    bias_out[...] = dot(found[: bias_out.shape[0]], table[...].astype(jnp.bfloat16), NN).astype(jnp.bfloat16)


def mix(normed_q, bias, normed_k, member, values):
    factor = normed_q.shape[1] ** (-0.5) * math.log2(math.e)
    scores = dot(jnp.concatenate([normed_q, bias], axis=1), jnp.concatenate([normed_k, member], axis=1), NT)
    peak = jnp.max(scores, axis=1, keepdims=True)
    weights = jnp.exp2((scores - peak) * factor)
    denom = jnp.sum(weights, axis=1, keepdims=True)
    mixed = dot(weights.astype(jnp.bfloat16), values, NN)
    return (mixed / denom).astype(jnp.bfloat16)


def peer_kernel(n, half, streams, tok, heads, q_gain, *refs):
    keys, values, member, bias, out = refs[:n], refs[n : 2 * n], refs[2 * n : 2 * n + half], refs[2 * n + half : -1], refs[-1]
    first_head = lax.rem(lax.axis_index("head") * streams, heads) + lax.rem(lax.axis_index("seq"), 2) * half
    scale = scales_of(keys[1], 0).T[:, :1]
    for i in range(half):
        at = pl.ds(i * tok, tok)
        normed_k = jnp.concatenate([keys[m][at, :] for m in range(n)], axis=0)
        value_rows = jnp.concatenate([values[m][at, :] for m in range(n)], axis=0)
        raw = values[1][pl.ds((2 * streams - 3 * half + i) * tok, tok), :].astype(jnp.float32)
        normed_q = (raw * scale * q_gain[pl.ds(first_head + i, 1), :]).astype(jnp.bfloat16)
        out[i] = mix(normed_q, bias[i][tok:], normed_k, member[i][...], value_rows)


def scales_of(message, kind):
    rows = message[message.shape[0] - 16 :, :].astype(jnp.float32)
    row = (rows[3 * kind : 3 * kind + 1, :] + rows[3 * kind + 1 : 3 * kind + 2, :]) + rows[3 * kind + 2 : 3 * kind + 3, :]
    return jnp.concatenate([row] * 8, axis=0)


def own_kernel(n, half, kept, tok, heads, k_gain, own, *refs):
    keys, values, member, refs = refs[:n], refs[n : 2 * n], refs[2 * n : 2 * n + kept], refs[2 * n + kept :]
    bias, further, out = refs[:kept], dict(zip([m for m in range(n) if m & (m - 1)], refs[kept:-1])), refs[-1]
    streams = half + kept
    first_head = lax.rem(lax.axis_index("head") * streams, heads)
    if kept > half:
        scales = [None] + [scales_of(keys[m], 1).T[:, :1] for m in range(1, n)]
    for i in range(kept):
        at = pl.ds(i * tok, tok)
        if i < half:
            parts = [keys[m][at, :] for m in range(n)]
            value_rows = jnp.concatenate([values[m][at, :] for m in range(n)], axis=0)
        else:
            gain = k_gain[pl.ds(first_head + half + i, 1), :]
            parts, value_rows = [own[pl.ds((kept + i - half) * tok, tok), :]], []
            for m in range(n):
                ref, start = (values[m], half) if m & (m - 1) == 0 else (further[m], 0)
                start = (start + 2 * (i - half)) * tok
                value_rows.append(ref[start : start + tok, :])
                if m:
                    raw = ref[start + tok : start + 2 * tok, :].astype(jnp.float32)
                    parts.append((raw * scales[m] * gain).astype(jnp.bfloat16))
            value_rows = jnp.concatenate(value_rows, axis=0)
        out[i] = mix(own[at, :], bias[i][:tok], jnp.concatenate(parts, axis=0), member[i][...], value_rows)


def local(n, query, key, value, q_gain, k_gain, order, cluster_rows, block_map):
    streams, tok, width = query.shape
    heads = q_gain.shape[0]
    half = streams // 2
    rest = streams - 2 * half
    kept = half + rest
    block_count = block_map.shape[2]
    clusters = cluster_rows.shape[1]
    blocks_per = block_count // clusters
    padded = -(-block_count // LANES) * LANES
    bf16, f32 = jnp.bfloat16, jnp.float32
    head_size = lax.axis_size("head")

    def exchange(rows, m):
        return lax.ppermute(rows, "seq", [(i, i ^ m) for i in range(n)])

    def after(rows, done):
        return lax.optimization_barrier((rows, done))[0]

    tail = -(-2 * kept // 16) * 16
    sized = lambda count: pltpu.VMEM((count * tok + tail, width), bf16)
    note, v_same, v_other, v_plain = pl.pallas_call(
        functools.partial(prep_kernel, half, tail),
        out_shape=[pltpu.VMEM((8, tok), f32), sized(half + 2 * rest), sized(2 * half + 2 * rest), sized(half)],
        in_specs=[ANY] * 4,
        out_specs=[VMEM] * 4,
        scratch_shapes=[
            pltpu.VMEM(query.shape, bf16),
            pltpu.VMEM(key.shape, bf16),
            pltpu.VMEM(order.shape, jnp.int32),
            pltpu.SemaphoreType.DMA((3 + 4 * half + 4 * rest,)),
        ],
        compiler_params=limit,
    )(*[pltpu.with_memory_space_constraint(x, pltpu.HBM) for x in (query, key, value, order)])

    values, tables = [v_same] + [None] * (n - 1), [None] * kept

    chain = [2**i for i in range(max(heads // streams, 1).bit_length() - 1)]
    launches = [[] for _ in range(len(chain) + 1)]
    fillers = [[] for _ in range(len(chain) + 1)]
    for m in reversed(range(1, n)):
        launches[min(m % 2, len(chain))].append(m)
    for i in range(kept):
        fillers[min(1 + (i > 0), len(chain))].append(i)

    def beside(at, note):
        for m in launches[at]:
            message = v_other if m == 1 else v_plain if m % 2 else v_same
            values[m] = exchange(after(message, note) if at else message, m)
        for i in fillers[at]:
            tables[i] = call(
                functools.partial(table_kernel, half, i),
                jax.ShapeDtypeStruct((padded, padded), f32),
                [after(block_map, note)],
                cost=weight,
            )

    beside(0, note)
    for at, step in enumerate(chain):
        note = note + lax.ppermute(note, "head", [(i, i ^ step) for i in range(head_size)])
        beside(at + 1, note)
    rows = lambda count, more: jax.ShapeDtypeStruct((count * tok + more, width), bf16)
    k_same, k_other, own_rows = call(
        functools.partial(norm_kernel, half, heads),
        [rows(half, 16), rows(half, 16), rows(kept + rest, 0)],
        [note, query, key, q_gain, k_gain],
    )
    keys = [k_same] + [None] * (n - 1)
    for m in reversed(range(1, n)):
        message = k_other if m % 2 else k_same
        if m == 1 and n > 2:
            message = after(message, values[2])
        keys[m] = exchange(message, m)

    further, across = {}, n // 2
    held = {}
    while rest and across:
        group = sorted(held)
        if group:
            sent = held[group[0]] if len(group) == 1 else jnp.concatenate([held[m] for m in group], axis=0)
            got = exchange(sent, across)
            size = 2 * rest * tok
            for at, m in enumerate(group):
                held[m ^ across] = further[m ^ across] = got if len(group) == 1 else got[at * size : (at + 1) * size]
        held[across] = values[across][half * tok : (half + 2 * rest) * tok]
        across //= 2

    cluster_rows = after(cluster_rows, note)
    start = jnp.cumsum(cluster_rows, axis=1, dtype=jnp.int32) - cluster_rows
    step_rows = jnp.arange(blocks_per, dtype=jnp.int32) * BLOCK
    low = start[:, :, None] + step_rows
    high = jnp.minimum(low + BLOCK, (start + cluster_rows)[:, :, None])
    bounds = jnp.stack([low.reshape(streams, block_count), high.reshape(streams, block_count)], axis=1)
    bounds = jnp.pad(bounds.reshape(2 * streams, block_count).astype(f32), ((0, 0), (0, padded - block_count)))

    member, bias = [None] * kept, [None] * kept
    for i in range(kept):
        member[i], bias[i] = call(
            functools.partial(blocks_kernel, half, i),
            [
                jax.ShapeDtypeStruct((n * tok, padded), bf16),
                jax.ShapeDtypeStruct(((2 if i < half else 1) * tok, padded), bf16),
            ],
            [bounds, tables[i], *values],
        )
    peer = call(
        functools.partial(peer_kernel, n, half, streams, tok, heads),
        jax.ShapeDtypeStruct((half, tok, width), bf16),
        [q_gain, *keys, *values, *member[:half], *bias[:half]],
    )
    theirs = exchange(peer, 1)
    own = call(
        functools.partial(own_kernel, n, half, kept, tok, heads),
        jax.ShapeDtypeStruct((kept, tok, width), bf16),
        [k_gain, own_rows, *keys, *values, *member, *bias, *[further[m] for m in sorted(further)]],
    )
    even = lax.axis_index("seq") % 2 == 0
    lower = jnp.where(even, own[:half], theirs)
    upper = jnp.where(even, theirs, own[:half])
    return jnp.concatenate([lower, upper, own[half:]], axis=0)


def solution(mesh):
    return jax.shard_map(
        functools.partial(local, mesh.shape["seq"]),
        mesh=mesh,
        in_specs=(
            P("head", "seq", None),
            P("head", "seq", None),
            P("head", "seq", None),
            P(),
            P(),
            P("head", "seq"),
            P("head", None),
            P("head", None, None),
        ),
        out_specs=P("head", "seq", None),
        check_vma=False,
    )
```

```python
import functools
import math

import jax
import jax.numpy as jnp
from jax import lax
from jax.experimental import pallas as pl
from jax.experimental.pallas import tpu as pltpu
from jax.sharding import PartitionSpec as P

BLOCK = 128
LANES = 128
epsilon = 1e-06
far = -1e30
weight = 20_000_000_000

NT = (((1,), (1,)), ((), ()))
NN = (((1,), (0,)), ((), ()))
VMEM = pl.BlockSpec(memory_space=pltpu.VMEM)
ANY = pl.BlockSpec(memory_space=pl.ANY)
limit = pltpu.CompilerParams(vmem_limit_bytes=48 * 1024 * 1024)


def dot(a, b, dims, precision=None):
    return lax.dot_general(a, b, dims, precision=precision, preferred_element_type=jnp.float32)


def one_hot(hit):
    return hit.astype(jnp.float32).astype(jnp.bfloat16)


def call(body, shapes, args, cost=None, **more):
    return pl.pallas_call(
        body,
        out_shape=shapes,
        in_specs=[VMEM] * len(args),
        out_specs=jax.tree.map(lambda _: VMEM, shapes),
        compiler_params=limit,
        cost_estimate=cost and pl.CostEstimate(flops=cost, bytes_accessed=0, transcendentals=0),
        **more,
    )(*args)


def prep_kernel(half, early, tail, query, key, value, order, note, same, other, plain, q_in, k_in, order_in, sems):
    streams, tok, width = query.shape
    rest = streams - 2 * half
    parity = lax.rem(lax.axis_index("seq"), 2)
    pairs = [(ref.at[s], there.at[s]) for ref, there in ((query, q_in), (key, k_in)) for s in range(streams)]
    pairs.append((order, order_in))
    for target, side in ((plain, 1 - parity), (same, parity), (other, 1 - parity)):
        rows = [(value, side * half + i) for i in range(half)] + [(key, side * half + i) for i in range(early)]
        if target is not plain:
            for s in range(2 * half, streams):
                rows += [(value, s), (key, s)]
        if target is other:
            rows += [(query, side * half + i) for i in range(half)]
        pairs += [(ref.at[s], target.at[pl.ds(at * tok, tok)]) for at, (ref, s) in enumerate(rows)]
    copies = [pltpu.make_async_copy(src, dst, sems.at[i]) for i, (src, dst) in enumerate(pairs)]
    for copy in copies:
        copy.start()
    totals = []
    for j, ref in enumerate((q_in, k_in)):
        total = None
        for i in range(streams):
            copies[j * streams + i].wait()
            wide = ref[i].astype(jnp.float32)
            total = wide * wide if total is None else total + wide * wide
        totals.append(jnp.sum(total.T, axis=0, keepdims=True))
    row = lax.broadcasted_iota(jnp.int32, (8, tok), 0)
    note[...] = jnp.where(row == 0, totals[0], jnp.where(row == 1, totals[1], 0.0))
    copies[2 * streams].wait()
    row = lax.broadcasted_iota(jnp.int32, (tail, tok), 0)
    for side, targets in ((1 - parity, (plain, other)), (parity, (same,))):
        rows = jnp.zeros((tail, tok), jnp.float32)
        for i in range(streams - half):
            s = side * half + i if i < half else half + i
            ids = order_in[pl.ds(s, 1), :].astype(jnp.float32)
            high = jnp.floor(ids / tok)
            rows = jnp.where(row == 2 * i, high, jnp.where(row == 2 * i + 1, ids - high * tok, rows))
        for target in targets:
            target[target.shape[0] - tail :, :] = rows.astype(jnp.bfloat16)
    for copy in copies[2 * streams + 1 :]:
        copy.wait()


def norm_kernel(half, early, heads, totals, query, key, q_gain, k_gain, same, other, own):
    streams, tok, width = query.shape
    kept = streams - half
    parity = lax.rem(lax.axis_index("seq"), 2)
    first_head = lax.rem(lax.axis_index("head") * streams, heads)
    scales = lax.rsqrt(totals[...] / (heads * width) + epsilon)
    columns = scales.T

    def normal(ref, gains, s, column):
        gain = gains[pl.ds(first_head + s, 1), :]
        return (ref[s].astype(jnp.float32) * columns[:, column : column + 1] * gain).astype(jnp.bfloat16)

    row = lax.broadcasted_iota(jnp.int32, (16, tok), 0)
    rows = jnp.zeros((16, tok), jnp.float32)
    for j in range(2):
        piece = scales[j : j + 1, :]
        for i in range(3):
            cut = piece.astype(jnp.bfloat16).astype(jnp.float32)
            rows = jnp.where(row == 3 * j + i, cut, rows)
            piece = piece - cut
    rows = rows.astype(jnp.bfloat16)
    for target in (same, other):
        target[target.shape[0] - 16 :, :] = rows
    for i in range(half):
        mine, theirs = parity * half + i, (1 - parity) * half + i
        own[pl.ds(i * tok, tok), :] = normal(query, q_gain, mine, 0)
        if i < early:
            own[pl.ds((2 * kept - half + i) * tok, tok), :] = normal(key, k_gain, mine, 1)
        else:
            at = pl.ds((i - early) * tok, tok)
            same[at, :] = normal(key, k_gain, mine, 1)
            other[at, :] = normal(key, k_gain, theirs, 1)
    for s in range(2 * half, streams):
        own[pl.ds((s - half) * tok, tok), :] = normal(query, q_gain, s, 0)
        own[pl.ds((kept + s - 2 * half) * tok, tok), :] = normal(key, k_gain, s, 1)


def table_kernel(half, i, block_map, table):
    count = block_map.shape[1]
    s = lax.rem(lax.axis_index("seq"), 2) * half + i if i < half else half + i
    row = lax.broadcasted_iota(jnp.int32, (count, count), 0)
    column = lax.broadcasted_iota(jnp.int32, (count, count), 1)
    table[...] = jnp.zeros_like(table)
    table[:count, :count] = jnp.where((block_map[s] == 1) | (row == column), 0.0, far)


def blocks_kernel(half, i, bounds, table, *refs):
    notes, member, bias_out = refs[:-2], refs[-2], refs[-1]
    n = len(notes)
    tok = notes[0].shape[1]
    padded = bounds.shape[1]
    tail = notes[0].shape[0] % tok
    my_seq = lax.axis_index("seq")
    s = lax.rem(my_seq, 2) * half + i if i < half else half + i
    row_in = lax.broadcasted_iota(jnp.int32, (tok, LANES), 0)
    tokens = [(row_in + lax.bitwise_xor(my_seq, m) * tok).astype(jnp.float32) for m in range(n)]
    low = bounds[pl.ds(2 * s, 1), :]
    high = bounds[pl.ds(2 * s + 1, 1), :]
    blocks = []
    ids = []
    for m in range(n):
        wide = jnp.concatenate([tokens[m]] * (padded // LANES), axis=1)
        blocks.append(one_hot((low <= wide) & (wide < high)))
        rows = notes[m][notes[m].shape[0] - tail :, :].astype(jnp.float32)
        ids.append(rows[2 * i : 2 * i + 1, :] * tok + rows[2 * i + 1 : 2 * i + 2, :])
    place_block = jnp.concatenate(blocks, axis=0)
    hit = jnp.concatenate(
        [jnp.concatenate([one_hot(tokens[m] == ids[j]) for j in range(n)], axis=1) for m in range(n)], axis=0
    )
    found = dot(hit, place_block, NN).astype(jnp.bfloat16)
    member[...] = found
    bias_out[...] = dot(found[: bias_out.shape[0]], table[...].astype(jnp.bfloat16), NN).astype(jnp.bfloat16)


def mix(normed_q, bias, normed_k, member, values):
    factor = normed_q.shape[1] ** (-0.5) * math.log2(math.e)
    scores = dot(jnp.concatenate([normed_q, bias], axis=1), jnp.concatenate([normed_k, member], axis=1), NT)
    peak = jnp.max(scores, axis=1, keepdims=True)
    weights = jnp.exp2((scores - peak) * factor)
    denom = jnp.sum(weights, axis=1, keepdims=True)
    mixed = dot(weights.astype(jnp.bfloat16), values, NN)
    return (mixed / denom).astype(jnp.bfloat16)


def peer_kernel(n, half, early, streams, tok, heads, q_gain, k_gain, own, *refs):
    keys, values, refs = refs[:n], refs[n : 2 * n], refs[2 * n :]
    member, bias, (out, normed) = refs[:half], refs[half : 2 * half], refs[2 * half :]
    first_head = lax.rem(lax.axis_index("head") * streams, heads) + lax.rem(lax.axis_index("seq"), 2) * half
    scale_q = scales_of(keys[1], 0).T[:, :1]
    scale_k = [None] + [scales_of(keys[m], 1).T[:, :1] for m in range(1, n)]
    queries = values[1].shape[0] // tok - half
    for i in range(half):
        if i < early:
            gain = k_gain[pl.ds(first_head + i, 1), :]
            parts = [own[pl.ds((2 * streams - 3 * half + i) * tok, tok), :]]
            for m in range(1, n):
                raw = values[m][pl.ds((half + i) * tok, tok), :].astype(jnp.float32)
                parts.append((raw * scale_k[m] * gain).astype(jnp.bfloat16))
            normed_k = jnp.concatenate(parts, axis=0)
            normed[i] = normed_k
        else:
            normed_k = jnp.concatenate([keys[m][pl.ds((i - early) * tok, tok), :] for m in range(n)], axis=0)
        value_rows = jnp.concatenate([values[m][pl.ds(i * tok, tok), :] for m in range(n)], axis=0)
        raw = values[1][pl.ds((queries + i) * tok, tok), :].astype(jnp.float32)
        normed_q = (raw * scale_q * q_gain[pl.ds(first_head + i, 1), :]).astype(jnp.bfloat16)
        out[i] = mix(normed_q, bias[i][tok:], normed_k, member[i][...], value_rows)


def scales_of(message, kind):
    rows = message[message.shape[0] - 16 :, :].astype(jnp.float32)
    row = (rows[3 * kind : 3 * kind + 1, :] + rows[3 * kind + 1 : 3 * kind + 2, :]) + rows[3 * kind + 2 : 3 * kind + 3, :]
    return jnp.concatenate([row] * 8, axis=0)


def own_kernel(n, half, early, kept, tok, heads, k_gain, own, normed, *refs):
    keys, values, member, refs = refs[:n], refs[n : 2 * n], refs[2 * n : 2 * n + kept], refs[2 * n + kept :]
    bias, further, out = refs[:kept], dict(zip([m for m in range(n) if m & (m - 1)], refs[kept:-1])), refs[-1]
    streams = half + kept
    first_head = lax.rem(lax.axis_index("head") * streams, heads)
    if kept > half:
        scales = [None] + [scales_of(keys[m], 1).T[:, :1] for m in range(1, n)]
    for i in range(kept):
        at = pl.ds(i * tok, tok)
        if i < half:
            parts = [normed[i]] if i < early else [keys[m][pl.ds((i - early) * tok, tok), :] for m in range(n)]
            value_rows = jnp.concatenate([values[m][at, :] for m in range(n)], axis=0)
        else:
            gain = k_gain[pl.ds(first_head + half + i, 1), :]
            parts, value_rows = [own[pl.ds((kept + i - half) * tok, tok), :]], []
            for m in range(n):
                ref, start = (values[m], half + early) if m & (m - 1) == 0 else (further[m], 0)
                start = (start + 2 * (i - half)) * tok
                value_rows.append(ref[start : start + tok, :])
                if m:
                    raw = ref[start + tok : start + 2 * tok, :].astype(jnp.float32)
                    parts.append((raw * scales[m] * gain).astype(jnp.bfloat16))
            value_rows = jnp.concatenate(value_rows, axis=0)
        out[i] = mix(own[at, :], bias[i][:tok], jnp.concatenate(parts, axis=0), member[i][...], value_rows)


def local(n, query, key, value, q_gain, k_gain, order, cluster_rows, block_map):
    streams, tok, width = query.shape
    heads = q_gain.shape[0]
    half = streams // 2
    rest = streams - 2 * half
    kept = half + rest
    block_count = block_map.shape[2]
    clusters = cluster_rows.shape[1]
    blocks_per = block_count // clusters
    padded = -(-block_count // LANES) * LANES
    bf16, f32 = jnp.bfloat16, jnp.float32
    head_size = lax.axis_size("head")

    def exchange(rows, m):
        return lax.ppermute(rows, "seq", [(i, i ^ m) for i in range(n)])

    def after(rows, done):
        return lax.optimization_barrier((rows, done))[0]

    tail = -(-2 * kept // 16) * 16
    early = half - half // 2
    lead = half + early
    sized = lambda count: pltpu.VMEM((count * tok + tail, width), bf16)
    note, v_same, v_other, v_plain = pl.pallas_call(
        functools.partial(prep_kernel, half, early, tail),
        out_shape=[pltpu.VMEM((8, tok), f32), sized(lead + 2 * rest), sized(lead + 2 * rest + half), sized(lead)],
        in_specs=[ANY] * 4,
        out_specs=[VMEM] * 4,
        scratch_shapes=[
            pltpu.VMEM(query.shape, bf16),
            pltpu.VMEM(key.shape, bf16),
            pltpu.VMEM(order.shape, jnp.int32),
            pltpu.SemaphoreType.DMA((2 * streams + 1 + 3 * lead + 4 * rest + half,)),
        ],
        compiler_params=limit,
    )(*[pltpu.with_memory_space_constraint(x, pltpu.HBM) for x in (query, key, value, order)])

    values, tables = [v_same] + [None] * (n - 1), [None] * kept

    chain = [2**i for i in range(max(heads // streams, 1).bit_length() - 1)]
    launches = [[] for _ in range(len(chain) + 1)]
    fillers = [[] for _ in range(len(chain) + 1)]
    for m in reversed(range(1, n)):
        launches[min(m % 2, len(chain))].append(m)
    for i in range(kept):
        fillers[min(1 + (i > 0), len(chain))].append(i)

    def beside(at, note):
        for m in launches[at]:
            message = v_other if m == 1 else v_plain if m % 2 else v_same
            values[m] = exchange(after(message, note) if at else message, m)
        for i in fillers[at]:
            tables[i] = call(
                functools.partial(table_kernel, half, i),
                jax.ShapeDtypeStruct((padded, padded), f32),
                [after(block_map, note)],
                cost=weight,
            )

    beside(0, note)
    for at, step in enumerate(chain):
        note = note + lax.ppermute(note, "head", [(i, i ^ step) for i in range(head_size)])
        beside(at + 1, note)
    rows = lambda count, more: jax.ShapeDtypeStruct((count * tok + more, width), bf16)
    k_same, k_other, own_rows = call(
        functools.partial(norm_kernel, half, early, heads),
        [rows(half - early, 16), rows(half - early, 16), rows(kept + rest + early, 0)],
        [note, query, key, q_gain, k_gain],
    )
    keys = [k_same] + [None] * (n - 1)
    for m in reversed(range(1, n)):
        message = k_other if m % 2 else k_same
        if m <= 2 < n:
            message = after(message, values[2])
        keys[m] = exchange(message, m)

    further, across = {}, n // 2
    held = {}
    while rest and across:
        group = sorted(held)
        if group:
            sent = held[group[0]] if len(group) == 1 else jnp.concatenate([held[m] for m in group], axis=0)
            got = exchange(sent, across)
            size = 2 * rest * tok
            for at, m in enumerate(group):
                held[m ^ across] = further[m ^ across] = got if len(group) == 1 else got[at * size : (at + 1) * size]
        held[across] = values[across][lead * tok : (lead + 2 * rest) * tok]
        across //= 2

    cluster_rows = after(cluster_rows, note)
    start = jnp.cumsum(cluster_rows, axis=1, dtype=jnp.int32) - cluster_rows
    step_rows = jnp.arange(blocks_per, dtype=jnp.int32) * BLOCK
    low = start[:, :, None] + step_rows
    high = jnp.minimum(low + BLOCK, (start + cluster_rows)[:, :, None])
    bounds = jnp.stack([low.reshape(streams, block_count), high.reshape(streams, block_count)], axis=1)
    bounds = jnp.pad(bounds.reshape(2 * streams, block_count).astype(f32), ((0, 0), (0, padded - block_count)))

    member, bias = [None] * kept, [None] * kept
    for i in range(kept):
        member[i], bias[i] = call(
            functools.partial(blocks_kernel, half, i),
            [
                jax.ShapeDtypeStruct((n * tok, padded), bf16),
                jax.ShapeDtypeStruct(((2 if i < half else 1) * tok, padded), bf16),
            ],
            [bounds, tables[i], *values],
        )
    peer, normed = call(
        functools.partial(peer_kernel, n, half, early, streams, tok, heads),
        [
            jax.ShapeDtypeStruct((half, tok, width), bf16),
            jax.ShapeDtypeStruct((early, n * tok, width), bf16),
        ],
        [q_gain, k_gain, own_rows, *keys, *values, *member[:half], *bias[:half]],
    )
    theirs = exchange(peer, 1)
    own = call(
        functools.partial(own_kernel, n, half, early, kept, tok, heads),
        jax.ShapeDtypeStruct((kept, tok, width), bf16),
        [k_gain, own_rows, normed, *keys, *values, *member, *bias, *[further[m] for m in sorted(further)]],
    )
    even = lax.axis_index("seq") % 2 == 0
    lower = jnp.where(even, own[:half], theirs)
    upper = jnp.where(even, theirs, own[:half])
    return jnp.concatenate([lower, upper, own[half:]], axis=0)


def solution(mesh):
    return jax.shard_map(
        functools.partial(local, mesh.shape["seq"]),
        mesh=mesh,
        in_specs=(
            P("head", "seq", None),
            P("head", "seq", None),
            P("head", "seq", None),
            P(),
            P(),
            P("head", "seq"),
            P("head", None),
            P("head", None, None),
        ),
        out_specs=P("head", "seq", None),
        check_vma=False,
    )
```

```python
import functools
import math

import jax
import jax.numpy as jnp
from jax import lax
from jax.experimental import pallas as pl
from jax.experimental.pallas import tpu as pltpu
from jax.sharding import PartitionSpec as P

BLOCK = 128
LANES = 128
epsilon = 1e-06
far = -1e30
weight = 20_000_000_000

NT = (((1,), (1,)), ((), ()))
NN = (((1,), (0,)), ((), ()))
VMEM = pl.BlockSpec(memory_space=pltpu.VMEM)
ANY = pl.BlockSpec(memory_space=pl.ANY)
limit = pltpu.CompilerParams(vmem_limit_bytes=48 * 1024 * 1024)


def dot(a, b, dims, precision=None):
    return lax.dot_general(a, b, dims, precision=precision, preferred_element_type=jnp.float32)


def one_hot(hit):
    return hit.astype(jnp.float32).astype(jnp.bfloat16)


def call(body, shapes, args, cost=None, **more):
    return pl.pallas_call(
        body,
        out_shape=shapes,
        in_specs=[VMEM] * len(args),
        out_specs=jax.tree.map(lambda _: VMEM, shapes),
        compiler_params=limit,
        cost_estimate=cost and pl.CostEstimate(flops=cost, bytes_accessed=0, transcendentals=0),
        **more,
    )(*args)


def prep_kernel(half, early, tail, query, key, value, order, note, same, other, plain, q_in, k_in, order_in, sems):
    streams, tok, width = query.shape
    rest = streams - 2 * half
    parity = lax.rem(lax.axis_index("seq"), 2)
    pairs = [(ref.at[s], there.at[s]) for ref, there in ((query, q_in), (key, k_in)) for s in range(streams)]
    pairs.append((order, order_in))
    for target, side in ((plain, 1 - parity), (same, parity), (other, 1 - parity)):
        rows = [(value, side * half + i) for i in range(half)] + [(key, side * half + i) for i in range(early)]
        if target is same:
            for s in range(2 * half, streams):
                rows += [(value, s), (key, s)]
        if target is other:
            rows += [(query, side * half + i) for i in range(half)]
        pairs += [(ref.at[s], target.at[pl.ds(at * tok, tok)]) for at, (ref, s) in enumerate(rows)]
    copies = [pltpu.make_async_copy(src, dst, sems.at[i]) for i, (src, dst) in enumerate(pairs)]
    for copy in copies:
        copy.start()
    totals = []
    for j, ref in enumerate((q_in, k_in)):
        total = None
        for i in range(streams):
            copies[j * streams + i].wait()
            wide = ref[i].astype(jnp.float32)
            total = wide * wide if total is None else total + wide * wide
        totals.append(jnp.sum(total.T, axis=0, keepdims=True))
    row = lax.broadcasted_iota(jnp.int32, (8, tok), 0)
    note[...] = jnp.where(row == 0, totals[0], jnp.where(row == 1, totals[1], 0.0))
    copies[2 * streams].wait()
    row = lax.broadcasted_iota(jnp.int32, (tail, tok), 0)
    for side, targets in ((1 - parity, (plain, other)), (parity, (same,))):
        rows = jnp.zeros((tail, tok), jnp.float32)
        for i in range(streams - half):
            s = side * half + i if i < half else half + i
            ids = order_in[pl.ds(s, 1), :].astype(jnp.float32)
            high = jnp.floor(ids / tok)
            rows = jnp.where(row == 2 * i, high, jnp.where(row == 2 * i + 1, ids - high * tok, rows))
        for target in targets:
            target[target.shape[0] - tail :, :] = rows.astype(jnp.bfloat16)
    for copy in copies[2 * streams + 1 :]:
        copy.wait()


def norm_kernel(half, early, heads, totals, query, key, q_gain, k_gain, same, other, own):
    streams, tok, width = query.shape
    kept = streams - half
    parity = lax.rem(lax.axis_index("seq"), 2)
    first_head = lax.rem(lax.axis_index("head") * streams, heads)
    scales = lax.rsqrt(totals[...] / (heads * width) + epsilon)
    columns = scales.T

    def normal(ref, gains, s, column):
        gain = gains[pl.ds(first_head + s, 1), :]
        return (ref[s].astype(jnp.float32) * columns[:, column : column + 1] * gain).astype(jnp.bfloat16)

    row = lax.broadcasted_iota(jnp.int32, (16, tok), 0)
    rows = jnp.zeros((16, tok), jnp.float32)
    for j in range(2):
        piece = scales[j : j + 1, :]
        for i in range(3):
            cut = piece.astype(jnp.bfloat16).astype(jnp.float32)
            rows = jnp.where(row == 3 * j + i, cut, rows)
            piece = piece - cut
    rows = rows.astype(jnp.bfloat16)
    for target in (same, other):
        target[target.shape[0] - 16 :, :] = rows
    for i in range(half):
        mine, theirs = parity * half + i, (1 - parity) * half + i
        own[pl.ds(i * tok, tok), :] = normal(query, q_gain, mine, 0)
        if i < early:
            own[pl.ds((2 * kept - half + i) * tok, tok), :] = normal(key, k_gain, mine, 1)
        else:
            at = pl.ds((i - early) * tok, tok)
            same[at, :] = normal(key, k_gain, mine, 1)
            other[at, :] = normal(key, k_gain, theirs, 1)
    for s in range(2 * half, streams):
        own[pl.ds((s - half) * tok, tok), :] = normal(query, q_gain, s, 0)
        own[pl.ds((kept + s - 2 * half) * tok, tok), :] = normal(key, k_gain, s, 1)


def table_kernel(half, i, block_map, table):
    count = block_map.shape[1]
    s = lax.rem(lax.axis_index("seq"), 2) * half + i if i < half else half + i
    row = lax.broadcasted_iota(jnp.int32, (count, count), 0)
    column = lax.broadcasted_iota(jnp.int32, (count, count), 1)
    table[...] = jnp.zeros_like(table)
    table[:count, :count] = jnp.where((block_map[s] == 1) | (row == column), 0.0, far)


def blocks_of(half, i, bounds, notes):
    n = len(notes)
    tok = notes[0].shape[1]
    padded = bounds.shape[1]
    tail = notes[0].shape[0] % tok
    my_seq = lax.axis_index("seq")
    s = lax.rem(my_seq, 2) * half + i if i < half else half + i
    row_in = lax.broadcasted_iota(jnp.int32, (tok, LANES), 0)
    tokens = [(row_in + lax.bitwise_xor(my_seq, m) * tok).astype(jnp.float32) for m in range(n)]
    low = bounds[pl.ds(2 * s, 1), :]
    high = bounds[pl.ds(2 * s + 1, 1), :]
    blocks = []
    ids = []
    for m in range(n):
        wide = jnp.concatenate([tokens[m]] * (padded // LANES), axis=1)
        blocks.append(one_hot((low <= wide) & (wide < high)))
        rows = notes[m][notes[m].shape[0] - tail :, :].astype(jnp.float32)
        ids.append(rows[2 * i : 2 * i + 1, :] * tok + rows[2 * i + 1 : 2 * i + 2, :])
    hit = jnp.concatenate(
        [jnp.concatenate([one_hot(tokens[m] == ids[j]) for j in range(n)], axis=1) for m in range(n)], axis=0
    )
    return dot(hit, jnp.concatenate(blocks, axis=0), NN).astype(jnp.bfloat16)


def blocks_kernel(half, picks, bounds, *refs):
    tables, refs = refs[: len(picks)], refs[len(picks) :]
    notes, outs = refs[: -2 * len(picks)], refs[-2 * len(picks) :]
    found = [blocks_of(half, i, bounds, notes) for i in picks]
    for at in range(len(picks)):
        outs[2 * at][...] = found[at]
        count = outs[2 * at + 1].shape[0]
        outs[2 * at + 1][...] = dot(found[at][:count], tables[at][...].astype(jnp.bfloat16), NN).astype(jnp.bfloat16)


def mix_all(tasks):
    factor = tasks[0][0].shape[1] ** (-0.5) * math.log2(math.e)
    scores = []
    for normed_q, bias, normed_k, member, _ in tasks:
        scores.append(dot(jnp.concatenate([normed_q, bias], axis=1), jnp.concatenate([normed_k, member], axis=1), NT))
    peaks = [jnp.max(score, axis=1, keepdims=True) for score in scores]
    weights = [jnp.exp2((score - peak) * factor) for score, peak in zip(scores, peaks)]
    denoms = [jnp.sum(weight, axis=1, keepdims=True) for weight in weights]
    mixed = [dot(weight.astype(jnp.bfloat16), task[4], NN) for weight, task in zip(weights, tasks)]
    return [(rows / denom).astype(jnp.bfloat16) for rows, denom in zip(mixed, denoms)]


def peer_kernel(n, half, early, streams, tok, heads, q_gain, k_gain, own, *refs):
    keys, values, refs = refs[:n], refs[n : 2 * n], refs[2 * n :]
    member, bias, (out, normed) = refs[:half], refs[half : 2 * half], refs[2 * half :]
    first_head = lax.rem(lax.axis_index("head") * streams, heads) + lax.rem(lax.axis_index("seq"), 2) * half
    scale_q, *scale_k = columns_of([(keys[1], 0)] + [(keys[m], 1) for m in range(1, n)])
    scale_k = [None] + scale_k
    queries = values[1].shape[0] // tok - half
    tasks = []
    for i in range(half):
        if i < early:
            gain = k_gain[pl.ds(first_head + i, 1), :]
            parts = [own[pl.ds((2 * streams - 3 * half + i) * tok, tok), :]]
            for m in range(1, n):
                raw = values[m][pl.ds((half + i) * tok, tok), :].astype(jnp.float32)
                parts.append((raw * scale_k[m] * gain).astype(jnp.bfloat16))
            normed_k = jnp.concatenate(parts, axis=0)
            normed[i] = normed_k
        else:
            normed_k = jnp.concatenate([keys[m][pl.ds((i - early) * tok, tok), :] for m in range(n)], axis=0)
        value_rows = jnp.concatenate([values[m][pl.ds(i * tok, tok), :] for m in range(n)], axis=0)
        raw = values[1][pl.ds((queries + i) * tok, tok), :].astype(jnp.float32)
        normed_q = (raw * scale_q * q_gain[pl.ds(first_head + i, 1), :]).astype(jnp.bfloat16)
        tasks.append((normed_q, bias[i][tok:], normed_k, member[i][...], value_rows))
    for i, rows in enumerate(mix_all(tasks)):
        out[i] = rows


def columns_of(picks):
    rows = []
    for message, kind in picks:
        tail = message[message.shape[0] - 16 :, :].astype(jnp.float32)
        rows.append((tail[3 * kind : 3 * kind + 1, :] + tail[3 * kind + 1 : 3 * kind + 2, :]) + tail[3 * kind + 2 : 3 * kind + 3, :])
    columns = jnp.concatenate(rows + [rows[0]] * (-len(rows) % 8), axis=0).T
    return [columns[:, at : at + 1] for at in range(len(picks))]


def own_kernel(n, half, early, kept, tok, heads, k_gain, own, normed, *refs):
    keys, values, member, refs = refs[:n], refs[n : 2 * n], refs[2 * n : 2 * n + kept], refs[2 * n + kept :]
    bias, further, out = refs[:kept], refs[kept:-1], refs[-1]
    streams = half + kept
    tasks = []
    first_head = lax.rem(lax.axis_index("head") * streams, heads)
    if kept > half:
        scales = [None] + columns_of([(keys[m], 1) for m in range(1, n)])
    for i in range(kept):
        at = pl.ds(i * tok, tok)
        if i < half:
            parts = [normed[i]] if i < early else [keys[m][pl.ds((i - early) * tok, tok), :] for m in range(n)]
            value_rows = jnp.concatenate([values[m][at, :] for m in range(n)], axis=0)
        else:
            gain = k_gain[pl.ds(first_head + half + i, 1), :]
            parts, value_rows = [own[pl.ds((kept + i - half) * tok, tok), :]], []
            for m in range(n):
                ref, start = further[m], 0
                start = (start + 2 * (i - half)) * tok
                value_rows.append(ref[start : start + tok, :])
                if m:
                    raw = ref[start + tok : start + 2 * tok, :].astype(jnp.float32)
                    parts.append((raw * scales[m] * gain).astype(jnp.bfloat16))
            value_rows = jnp.concatenate(value_rows, axis=0)
        tasks.append((own[at, :], bias[i][:tok], jnp.concatenate(parts, axis=0), member[i][...], value_rows))
    for i, rows in enumerate(mix_all(tasks)):
        out[i] = rows


def local(n, query, key, value, q_gain, k_gain, order, cluster_rows, block_map):
    streams, tok, width = query.shape
    heads = q_gain.shape[0]
    half = streams // 2
    rest = streams - 2 * half
    kept = half + rest
    block_count = block_map.shape[2]
    clusters = cluster_rows.shape[1]
    blocks_per = block_count // clusters
    padded = -(-block_count // LANES) * LANES
    bf16, f32 = jnp.bfloat16, jnp.float32
    head_size = lax.axis_size("head")

    def exchange(rows, m):
        return lax.ppermute(rows, "seq", [(i, i ^ m) for i in range(n)])

    def after(rows, done):
        return lax.optimization_barrier((rows, done))[0]

    tail = -(-2 * kept // 16) * 16
    early = half - half // 2
    lead = half + early
    sized = lambda count: pltpu.VMEM((count * tok + tail, width), bf16)
    note, v_same, v_other, v_plain = pl.pallas_call(
        functools.partial(prep_kernel, half, early, tail),
        out_shape=[pltpu.VMEM((8, tok), f32), sized(lead + 2 * rest), sized(lead + half), sized(lead)],
        in_specs=[ANY] * 4,
        out_specs=[VMEM] * 4,
        scratch_shapes=[
            pltpu.VMEM(query.shape, bf16),
            pltpu.VMEM(key.shape, bf16),
            pltpu.VMEM(order.shape, jnp.int32),
            pltpu.SemaphoreType.DMA((2 * streams + 1 + 3 * lead + 2 * rest + half,)),
        ],
        compiler_params=limit,
    )(*[pltpu.with_memory_space_constraint(x, pltpu.HBM) for x in (query, key, value, order)])

    values, tables = [v_same] + [None] * (n - 1), [None] * kept

    chain = [2**i for i in range(max(heads // streams, 1).bit_length() - 1)]
    launches = [[] for _ in range(len(chain) + 1)]
    fillers = [[] for _ in range(len(chain) + 1)]
    for m in reversed(range(1, n)):
        launches[min(0 if m % 2 == 0 else 1 if m == 1 else 2, len(chain))].append(m)
    for i in range(kept):
        fillers[min(i, len(chain))].append(i)

    def beside(at, note):
        for m in launches[at]:
            message = v_other if m == 1 else v_plain if m % 2 else v_same
            values[m] = exchange(after(message, note) if at else message, m)
        for i in fillers[at]:
            tables[i] = call(
                functools.partial(table_kernel, half, i),
                jax.ShapeDtypeStruct((padded, padded), f32),
                [after(block_map, note)],
                cost=weight,
            )

    beside(0, note)
    for at, step in enumerate(chain):
        note = note + lax.ppermute(note, "head", [(i, i ^ step) for i in range(head_size)])
        beside(at + 1, note)
    rows = lambda count, more: jax.ShapeDtypeStruct((count * tok + more, width), bf16)
    k_same, k_other, own_rows = call(
        functools.partial(norm_kernel, half, early, heads),
        [rows(half - early, 16), rows(half - early, 16), rows(kept + rest + early, 0)],
        [note, query, key, q_gain, k_gain],
    )
    keys = [k_same] + [None] * (n - 1)
    for m in reversed(range(1, n)):
        message = k_other if m % 2 else k_same
        keys[m] = exchange(message, m)

    cluster_rows = after(cluster_rows, note)
    start = jnp.cumsum(cluster_rows, axis=1, dtype=jnp.int32) - cluster_rows
    step_rows = jnp.arange(blocks_per, dtype=jnp.int32) * BLOCK
    low = start[:, :, None] + step_rows
    high = jnp.minimum(low + BLOCK, (start + cluster_rows)[:, :, None])
    bounds = jnp.stack([low.reshape(streams, block_count), high.reshape(streams, block_count)], axis=1)
    bounds = jnp.pad(bounds.reshape(2 * streams, block_count).astype(f32), ((0, 0), (0, padded - block_count)))

    member, bias = [None] * kept, [None] * kept
    for picks in [list(range(half)), list(range(half, kept))][: 1 + (rest > 0)]:
        shapes = []
        for i in picks:
            shapes.append(jax.ShapeDtypeStruct((n * tok, padded), bf16))
            shapes.append(jax.ShapeDtypeStruct(((2 if i < half else 1) * tok, padded), bf16))
        made = call(
            functools.partial(blocks_kernel, half, picks),
            shapes,
            [bounds, *[tables[i] for i in picks], *values],
        )
        for at, i in enumerate(picks):
            member[i], bias[i] = made[2 * at], made[2 * at + 1]
    across = n // 2
    held = {0: values[0][lead * tok : (lead + 2 * rest) * tok]}
    while rest and across:
        if across == n // 2 and n > 2:
            held[across] = values[across][lead * tok : (lead + 2 * rest) * tok]
        else:
            group = sorted(held)
            sent = jnp.concatenate([held[m] for m in group], axis=0)
            got = exchange(after(sent, member[0]), across)
            size = 2 * rest * tok
            for at, m in enumerate(group):
                held[m ^ across] = got[at * size : (at + 1) * size]
        across //= 2
    further = held if rest else {}

    peer, normed = call(
        functools.partial(peer_kernel, n, half, early, streams, tok, heads),
        [
            jax.ShapeDtypeStruct((half, tok, width), bf16),
            jax.ShapeDtypeStruct((early, n * tok, width), bf16),
        ],
        [q_gain, k_gain, own_rows, *keys, *values, *member[:half], *bias[:half]],
    )
    theirs = exchange(peer, 1)
    own = call(
        functools.partial(own_kernel, n, half, early, kept, tok, heads),
        jax.ShapeDtypeStruct((kept, tok, width), bf16),
        [k_gain, own_rows, normed, *keys, *values, *member, *bias, *[further[m] for m in sorted(further)]],
    )
    even = lax.axis_index("seq") % 2 == 0
    lower = jnp.where(even, own[:half], theirs)
    upper = jnp.where(even, theirs, own[:half])
    return jnp.concatenate([lower, upper, own[half:]], axis=0)


def solution(mesh):
    return jax.shard_map(
        functools.partial(local, mesh.shape["seq"]),
        mesh=mesh,
        in_specs=(
            P("head", "seq", None),
            P("head", "seq", None),
            P("head", "seq", None),
            P(),
            P(),
            P("head", "seq"),
            P("head", None),
            P("head", None, None),
        ),
        out_specs=P("head", "seq", None),
        check_vma=False,
    )
```

```python
import functools
import math

import jax
import jax.numpy as jnp
from jax import lax
from jax.experimental import pallas as pl
from jax.experimental.pallas import tpu as pltpu
from jax.sharding import PartitionSpec as P

BLOCK = 128
LANES = 128
epsilon = 1e-06
far = -1e30
weight = 20_000_000_000

NT = (((1,), (1,)), ((), ()))
NN = (((1,), (0,)), ((), ()))
VMEM = pl.BlockSpec(memory_space=pltpu.VMEM)
ANY = pl.BlockSpec(memory_space=pl.ANY)
limit = pltpu.CompilerParams(vmem_limit_bytes=48 * 1024 * 1024)


def dot(a, b, dims, precision=None):
    return lax.dot_general(a, b, dims, precision=precision, preferred_element_type=jnp.float32)


def one_hot(hit):
    return hit.astype(jnp.float32).astype(jnp.bfloat16)


def call(body, shapes, args, cost=None, **more):
    return pl.pallas_call(
        body,
        out_shape=shapes,
        in_specs=[VMEM] * len(args),
        out_specs=jax.tree.map(lambda _: VMEM, shapes),
        compiler_params=limit,
        cost_estimate=cost and pl.CostEstimate(flops=cost, bytes_accessed=0, transcendentals=0),
        **more,
    )(*args)


def prep_kernel(half, early, tail, query, key, value, order, note, same, other, plain, q_in, k_in, order_in, sems):
    streams, tok, width = query.shape
    rest = streams - 2 * half
    parity = lax.rem(lax.axis_index("seq"), 2)
    pairs = [(order, order_in)]
    pairs += [(ref.at[s], there.at[s]) for ref, there in ((query, q_in), (key, k_in)) for s in range(streams)]
    for target, side in ((plain, 1 - parity), (same, parity), (other, 1 - parity)):
        rows = [(value, side * half + i) for i in range(half)] + [(key, side * half + i) for i in range(early)]
        if target is same:
            for s in range(2 * half, streams):
                rows += [(value, s), (key, s)]
        if target is other:
            rows += [(query, side * half + i) for i in range(half)]
        pairs += [(ref.at[s], target.at[pl.ds(at * tok, tok)]) for at, (ref, s) in enumerate(rows)]
    copies = [pltpu.make_async_copy(src, dst, sems.at[i]) for i, (src, dst) in enumerate(pairs)]
    for copy in copies:
        copy.start()
    copies[0].wait()
    row = lax.broadcasted_iota(jnp.int32, (tail, tok), 0)
    for side, targets in ((1 - parity, (plain, other)), (parity, (same,))):
        rows = jnp.zeros((tail, tok), jnp.float32)
        for i in range(streams - half):
            s = side * half + i if i < half else half + i
            ids = order_in[pl.ds(s, 1), :].astype(jnp.float32)
            high = jnp.floor(ids / tok)
            rows = jnp.where(row == 2 * i, high, jnp.where(row == 2 * i + 1, ids - high * tok, rows))
        for target in targets:
            target[target.shape[0] - tail :, :] = rows.astype(jnp.bfloat16)
    totals = []
    for j, ref in enumerate((q_in, k_in)):
        total = None
        for i in range(streams):
            copies[1 + j * streams + i].wait()
            wide = ref[i].astype(jnp.float32)
            total = wide * wide if total is None else total + wide * wide
        totals.append(jnp.sum(total.T, axis=0, keepdims=True))
    row = lax.broadcasted_iota(jnp.int32, (8, tok), 0)
    note[...] = jnp.where(row == 0, totals[0], jnp.where(row == 1, totals[1], 0.0))
    for copy in copies[2 * streams + 1 :]:
        copy.wait()


def norm_kernel(half, early, heads, totals, query, key, q_gain, k_gain, same, other, own):
    streams, tok, width = query.shape
    kept = streams - half
    parity = lax.rem(lax.axis_index("seq"), 2)
    first_head = lax.rem(lax.axis_index("head") * streams, heads)
    scales = lax.rsqrt(totals[...] / (heads * width) + epsilon)
    columns = scales.T

    def normal(ref, gains, s, column):
        gain = gains[pl.ds(first_head + s, 1), :]
        return (ref[s].astype(jnp.float32) * columns[:, column : column + 1] * gain).astype(jnp.bfloat16)

    row = lax.broadcasted_iota(jnp.int32, (16, tok), 0)
    rows = jnp.zeros((16, tok), jnp.float32)
    for j in range(2):
        piece = scales[j : j + 1, :]
        for i in range(3):
            cut = piece.astype(jnp.bfloat16).astype(jnp.float32)
            rows = jnp.where(row == 3 * j + i, cut, rows)
            piece = piece - cut
    rows = rows.astype(jnp.bfloat16)
    for target in (same, other):
        target[target.shape[0] - 16 :, :] = rows
    for i in range(half):
        mine, theirs = parity * half + i, (1 - parity) * half + i
        own[pl.ds(i * tok, tok), :] = normal(query, q_gain, mine, 0)
        if i < early:
            own[pl.ds((2 * kept - half + i) * tok, tok), :] = normal(key, k_gain, mine, 1)
        else:
            at = pl.ds((i - early) * tok, tok)
            same[at, :] = normal(key, k_gain, mine, 1)
            other[at, :] = normal(key, k_gain, theirs, 1)
    for s in range(2 * half, streams):
        own[pl.ds((s - half) * tok, tok), :] = normal(query, q_gain, s, 0)
        own[pl.ds((kept + s - 2 * half) * tok, tok), :] = normal(key, k_gain, s, 1)


def table_kernel(half, i, block_map, table):
    count = block_map.shape[1]
    s = lax.rem(lax.axis_index("seq"), 2) * half + i if i < half else half + i
    row = lax.broadcasted_iota(jnp.int32, (count, count), 0)
    column = lax.broadcasted_iota(jnp.int32, (count, count), 1)
    table[...] = jnp.zeros_like(table)
    table[:count, :count] = jnp.where((block_map[s] == 1) | (row == column), 0.0, far)


def blocks_of(half, i, bounds, notes):
    n = len(notes)
    tok = notes[0].shape[1]
    padded = bounds.shape[1]
    tail = notes[0].shape[0] % tok
    my_seq = lax.axis_index("seq")
    s = lax.rem(my_seq, 2) * half + i if i < half else half + i
    row_in = lax.broadcasted_iota(jnp.int32, (tok, LANES), 0)
    tokens = [(row_in + lax.bitwise_xor(my_seq, m) * tok).astype(jnp.float32) for m in range(n)]
    low = bounds[pl.ds(2 * s, 1), :]
    high = bounds[pl.ds(2 * s + 1, 1), :]
    blocks = []
    ids = []
    for m in range(n):
        wide = jnp.concatenate([tokens[m]] * (padded // LANES), axis=1)
        blocks.append(one_hot((low <= wide) & (wide < high)))
        rows = notes[m][notes[m].shape[0] - tail :, :].astype(jnp.float32)
        ids.append(rows[2 * i : 2 * i + 1, :] * tok + rows[2 * i + 1 : 2 * i + 2, :])
    hit = jnp.concatenate(
        [jnp.concatenate([one_hot(tokens[m] == ids[j]) for j in range(n)], axis=1) for m in range(n)], axis=0
    )
    return dot(hit, jnp.concatenate(blocks, axis=0), NN).astype(jnp.bfloat16)


def blocks_kernel(half, picks, bounds, *refs):
    tables, refs = refs[: len(picks)], refs[len(picks) :]
    notes, outs = refs[: -2 * len(picks)], refs[-2 * len(picks) :]
    found = [blocks_of(half, i, bounds, notes) for i in picks]
    for at in range(len(picks)):
        outs[2 * at][...] = found[at]
        count = outs[2 * at + 1].shape[0]
        outs[2 * at + 1][...] = dot(found[at][:count], tables[at][...].astype(jnp.bfloat16), NN).astype(jnp.bfloat16)


def mix_all(tasks):
    factor = tasks[0][0].shape[1] ** (-0.5) * math.log2(math.e)
    scores = []
    for normed_q, bias, normed_k, member, _ in tasks:
        scores.append(dot(jnp.concatenate([normed_q, bias], axis=1), jnp.concatenate([normed_k, member], axis=1), NT))
    peaks = [jnp.max(score, axis=1, keepdims=True) for score in scores]
    weights = [jnp.exp2((score - peak) * factor) for score, peak in zip(scores, peaks)]
    denoms = [jnp.sum(weight, axis=1, keepdims=True) for weight in weights]
    mixed = [dot(weight.astype(jnp.bfloat16), task[4], NN) for weight, task in zip(weights, tasks)]
    return [(rows / denom).astype(jnp.bfloat16) for rows, denom in zip(mixed, denoms)]


def peer_kernel(n, half, early, streams, tok, heads, q_gain, k_gain, own, *refs):
    keys, values, refs = refs[:n], refs[n : 2 * n], refs[2 * n :]
    member, bias, (out, normed) = refs[:half], refs[half : 2 * half], refs[2 * half :]
    first_head = lax.rem(lax.axis_index("head") * streams, heads) + lax.rem(lax.axis_index("seq"), 2) * half
    scale_q, *scale_k = columns_of([(keys[1], 0)] + [(keys[m], 1) for m in range(1, n)])
    scale_k = [None] + scale_k
    queries = values[1].shape[0] // tok - half
    tasks = []
    for i in range(half):
        if i < early:
            gain = k_gain[pl.ds(first_head + i, 1), :]
            parts = [own[pl.ds((2 * streams - 3 * half + i) * tok, tok), :]]
            for m in range(1, n):
                raw = values[m][pl.ds((half + i) * tok, tok), :].astype(jnp.float32)
                parts.append((raw * scale_k[m] * gain).astype(jnp.bfloat16))
            normed_k = jnp.concatenate(parts, axis=0)
            normed[i] = normed_k
        else:
            normed_k = jnp.concatenate([keys[m][pl.ds((i - early) * tok, tok), :] for m in range(n)], axis=0)
        value_rows = jnp.concatenate([values[m][pl.ds(i * tok, tok), :] for m in range(n)], axis=0)
        raw = values[1][pl.ds((queries + i) * tok, tok), :].astype(jnp.float32)
        normed_q = (raw * scale_q * q_gain[pl.ds(first_head + i, 1), :]).astype(jnp.bfloat16)
        tasks.append((normed_q, bias[i][tok:], normed_k, member[i][...], value_rows))
    for i, rows in enumerate(mix_all(tasks)):
        out[i] = rows


def columns_of(picks):
    rows = []
    for message, kind in picks:
        tail = message[message.shape[0] - 16 :, :].astype(jnp.float32)
        rows.append((tail[3 * kind : 3 * kind + 1, :] + tail[3 * kind + 1 : 3 * kind + 2, :]) + tail[3 * kind + 2 : 3 * kind + 3, :])
    columns = jnp.concatenate(rows + [rows[0]] * (-len(rows) % 8), axis=0).T
    return [columns[:, at : at + 1] for at in range(len(picks))]


def own_kernel(n, half, early, kept, tok, heads, k_gain, own, normed, *refs):
    keys, values, member, refs = refs[:n], refs[n : 2 * n], refs[2 * n : 2 * n + kept], refs[2 * n + kept :]
    bias, further, out = refs[:kept], refs[kept:-1], refs[-1]
    streams = half + kept
    tasks = []
    first_head = lax.rem(lax.axis_index("head") * streams, heads)
    if kept > half:
        scales = [None] + columns_of([(keys[m], 1) for m in range(1, n)])
    for i in range(kept):
        at = pl.ds(i * tok, tok)
        if i < half:
            parts = [normed[i]] if i < early else [keys[m][pl.ds((i - early) * tok, tok), :] for m in range(n)]
            value_rows = jnp.concatenate([values[m][at, :] for m in range(n)], axis=0)
        else:
            gain = k_gain[pl.ds(first_head + half + i, 1), :]
            parts, value_rows = [own[pl.ds((kept + i - half) * tok, tok), :]], []
            for m in range(n):
                ref, start = further[m], 0
                start = (start + 2 * (i - half)) * tok
                value_rows.append(ref[start : start + tok, :])
                if m:
                    raw = ref[start + tok : start + 2 * tok, :].astype(jnp.float32)
                    parts.append((raw * scales[m] * gain).astype(jnp.bfloat16))
            value_rows = jnp.concatenate(value_rows, axis=0)
        tasks.append((own[at, :], bias[i][:tok], jnp.concatenate(parts, axis=0), member[i][...], value_rows))
    for i, rows in enumerate(mix_all(tasks)):
        out[i] = rows


def local(n, query, key, value, q_gain, k_gain, order, cluster_rows, block_map):
    streams, tok, width = query.shape
    heads = q_gain.shape[0]
    half = streams // 2
    rest = streams - 2 * half
    kept = half + rest
    block_count = block_map.shape[2]
    clusters = cluster_rows.shape[1]
    blocks_per = block_count // clusters
    padded = -(-block_count // LANES) * LANES
    bf16, f32 = jnp.bfloat16, jnp.float32
    head_size = lax.axis_size("head")

    def exchange(rows, m):
        return lax.ppermute(rows, "seq", [(i, i ^ m) for i in range(n)])

    def after(rows, done):
        return lax.optimization_barrier((rows, done))[0]

    tail = -(-2 * kept // 16) * 16
    early = half - half // 2
    lead = half + early
    sized = lambda count: pltpu.VMEM((count * tok + tail, width), bf16)
    note, v_same, v_other, v_plain = pl.pallas_call(
        functools.partial(prep_kernel, half, early, tail),
        out_shape=[pltpu.VMEM((8, tok), f32), sized(lead + 2 * rest), sized(lead + half), sized(lead)],
        in_specs=[ANY] * 4,
        out_specs=[VMEM] * 4,
        scratch_shapes=[
            pltpu.VMEM(query.shape, bf16),
            pltpu.VMEM(key.shape, bf16),
            pltpu.VMEM(order.shape, jnp.int32),
            pltpu.SemaphoreType.DMA((2 * streams + 1 + 3 * lead + 2 * rest + half,)),
        ],
        compiler_params=limit,
    )(*[pltpu.with_memory_space_constraint(x, pltpu.HBM) for x in (query, key, value, order)])

    values, tables = [v_same] + [None] * (n - 1), [None] * kept

    chain = [2**i for i in range(max(heads // streams, 1).bit_length() - 1)]
    launches = [[] for _ in range(len(chain) + 1)]
    fillers = [[] for _ in range(len(chain) + 1)]
    for m in reversed(range(1, n)):
        launches[min(0 if m % 2 == 0 else 1 if m == 1 else 2, len(chain))].append(m)
    for i in range(kept):
        fillers[min(i, len(chain))].append(i)

    def beside(at, note):
        for m in launches[at]:
            message = v_other if m == 1 else v_plain if m % 2 else v_same
            values[m] = exchange(after(message, note) if at else message, m)
        for i in fillers[at]:
            tables[i] = call(
                functools.partial(table_kernel, half, i),
                jax.ShapeDtypeStruct((padded, padded), f32),
                [after(block_map, note)],
                cost=weight,
            )

    beside(0, note)
    for at, step in enumerate(chain):
        note = note + lax.ppermute(note, "head", [(i, i ^ step) for i in range(head_size)])
        beside(at + 1, note)
    rows = lambda count, more: jax.ShapeDtypeStruct((count * tok + more, width), bf16)
    k_same, k_other, own_rows = call(
        functools.partial(norm_kernel, half, early, heads),
        [rows(half - early, 16), rows(half - early, 16), rows(kept + rest + early, 0)],
        [note, query, key, q_gain, k_gain],
    )
    keys = [k_same] + [None] * (n - 1)
    for m in reversed(range(1, n)):
        message = k_other if m % 2 else k_same
        keys[m] = exchange(message, m)

    cluster_rows = after(cluster_rows, note)
    start = jnp.cumsum(cluster_rows, axis=1, dtype=jnp.int32) - cluster_rows
    step_rows = jnp.arange(blocks_per, dtype=jnp.int32) * BLOCK
    low = start[:, :, None] + step_rows
    high = jnp.minimum(low + BLOCK, (start + cluster_rows)[:, :, None])
    bounds = jnp.stack([low.reshape(streams, block_count), high.reshape(streams, block_count)], axis=1)
    bounds = jnp.pad(bounds.reshape(2 * streams, block_count).astype(f32), ((0, 0), (0, padded - block_count)))

    member, bias = [None] * kept, [None] * kept
    for picks in [list(range(half)), list(range(half, kept))][: 1 + (rest > 0)]:
        shapes = []
        for i in picks:
            shapes.append(jax.ShapeDtypeStruct((n * tok, padded), bf16))
            shapes.append(jax.ShapeDtypeStruct(((2 if i < half else 1) * tok, padded), bf16))
        made = call(
            functools.partial(blocks_kernel, half, picks),
            shapes,
            [bounds, *[tables[i] for i in picks], *values],
        )
        for at, i in enumerate(picks):
            member[i], bias[i] = made[2 * at], made[2 * at + 1]
    across = n // 2
    held = {0: values[0][lead * tok : (lead + 2 * rest) * tok]}
    while rest and across:
        if across == n // 2 and n > 2:
            held[across] = values[across][lead * tok : (lead + 2 * rest) * tok]
        else:
            group = sorted(held)
            sent = jnp.concatenate([held[m] for m in group], axis=0)
            got = exchange(after(sent, member[0]), across)
            size = 2 * rest * tok
            for at, m in enumerate(group):
                held[m ^ across] = got[at * size : (at + 1) * size]
        across //= 2
    further = held if rest else {}

    peer, normed = call(
        functools.partial(peer_kernel, n, half, early, streams, tok, heads),
        [
            jax.ShapeDtypeStruct((half, tok, width), bf16),
            jax.ShapeDtypeStruct((early, n * tok, width), bf16),
        ],
        [q_gain, k_gain, own_rows, *keys, *values, *member[:half], *bias[:half]],
    )
    theirs = exchange(peer, 1)
    own = call(
        functools.partial(own_kernel, n, half, early, kept, tok, heads),
        jax.ShapeDtypeStruct((kept, tok, width), bf16),
        [k_gain, own_rows, normed, *keys, *values, *member, *bias, *[further[m] for m in sorted(further)]],
    )
    even = lax.axis_index("seq") % 2 == 0
    lower = jnp.where(even, own[:half], theirs)
    upper = jnp.where(even, theirs, own[:half])
    return jnp.concatenate([lower, upper, own[half:]], axis=0)


def solution(mesh):
    return jax.shard_map(
        functools.partial(local, mesh.shape["seq"]),
        mesh=mesh,
        in_specs=(
            P("head", "seq", None),
            P("head", "seq", None),
            P("head", "seq", None),
            P(),
            P(),
            P("head", "seq"),
            P("head", None),
            P("head", None, None),
        ),
        out_specs=P("head", "seq", None),
        check_vma=False,
    )
```

```python
import functools
import math

import jax
import jax.numpy as jnp
from jax import lax
from jax.experimental import pallas as pl
from jax.experimental.pallas import tpu as pltpu
from jax.sharding import PartitionSpec as P

BLOCK = 128
LANES = 128
epsilon = 1e-06
far = -1e30
weight = 20_000_000_000

NT = (((1,), (1,)), ((), ()))
NN = (((1,), (0,)), ((), ()))
VMEM = pl.BlockSpec(memory_space=pltpu.VMEM)
ANY = pl.BlockSpec(memory_space=pl.ANY)
limit = pltpu.CompilerParams(vmem_limit_bytes=48 * 1024 * 1024)


def dot(a, b, dims, precision=None):
    return lax.dot_general(a, b, dims, precision=precision, preferred_element_type=jnp.float32)


def one_hot(hit):
    return hit.astype(jnp.float32).astype(jnp.bfloat16)


def call(body, shapes, args, cost=None, **more):
    return pl.pallas_call(
        body,
        out_shape=shapes,
        in_specs=[VMEM] * len(args),
        out_specs=jax.tree.map(lambda _: VMEM, shapes),
        compiler_params=limit,
        cost_estimate=cost and pl.CostEstimate(flops=cost, bytes_accessed=0, transcendentals=0),
        **more,
    )(*args)


def prep_kernel(half, early, tail, query, key, value, order, note, same, other, plain, q_in, k_in, order_in, sems):
    streams, tok, width = query.shape
    rest = streams - 2 * half
    parity = lax.rem(lax.axis_index("seq"), 2)
    pairs = [(order, order_in)]
    pairs += [(ref.at[s], there.at[s]) for ref, there in ((query, q_in), (key, k_in)) for s in range(streams)]
    for target, side in ((plain, 1 - parity), (same, parity), (other, 1 - parity)):
        rows = [(value, side * half + i) for i in range(half)] + [(key, side * half + i) for i in range(early)]
        if target is same:
            for s in range(2 * half, streams):
                rows += [(value, s), (key, s)]
        if target is other:
            rows += [(query, side * half + i) for i in range(half)]
        pairs += [(ref.at[s], target.at[pl.ds(at * tok, tok)]) for at, (ref, s) in enumerate(rows)]
    copies = [pltpu.make_async_copy(src, dst, sems.at[i]) for i, (src, dst) in enumerate(pairs)]
    for copy in copies:
        copy.start()
    copies[0].wait()
    row = lax.broadcasted_iota(jnp.int32, (tail, tok), 0)
    for side, targets in ((1 - parity, (plain, other)), (parity, (same,))):
        rows = jnp.zeros((tail, tok), jnp.float32)
        for i in range(streams - half):
            s = side * half + i if i < half else half + i
            ids = order_in[pl.ds(s, 1), :].astype(jnp.float32)
            high = jnp.floor(ids / tok)
            rows = jnp.where(row == 2 * i, high, jnp.where(row == 2 * i + 1, ids - high * tok, rows))
        for target in targets:
            target[target.shape[0] - tail :, :] = rows.astype(jnp.bfloat16)
    totals = []
    for j, ref in enumerate((q_in, k_in)):
        total = None
        for i in range(streams):
            copies[1 + j * streams + i].wait()
            wide = ref[i].astype(jnp.float32)
            total = wide * wide if total is None else total + wide * wide
        totals.append(jnp.sum(total.T, axis=0, keepdims=True))
    row = lax.broadcasted_iota(jnp.int32, (8, tok), 0)
    note[...] = jnp.where(row == 0, totals[0], jnp.where(row == 1, totals[1], 0.0))
    for copy in copies[2 * streams + 1 :]:
        copy.wait()


def norm_kernel(half, early, heads, totals, query, key, q_gain, k_gain, same, other, own):
    streams, tok, width = query.shape
    kept = streams - half
    parity = lax.rem(lax.axis_index("seq"), 2)
    first_head = lax.rem(lax.axis_index("head") * streams, heads)
    scales = lax.rsqrt(totals[...] / (heads * width) + epsilon)
    columns = scales.T

    def normal(ref, gains, s, column):
        gain = gains[pl.ds(first_head + s, 1), :]
        return (ref[s].astype(jnp.float32) * columns[:, column : column + 1] * gain).astype(jnp.bfloat16)

    row = lax.broadcasted_iota(jnp.int32, (16, tok), 0)
    rows = jnp.zeros((16, tok), jnp.float32)
    for j in range(2):
        piece = scales[j : j + 1, :]
        for i in range(3):
            cut = piece.astype(jnp.bfloat16).astype(jnp.float32)
            rows = jnp.where(row == 3 * j + i, cut, rows)
            piece = piece - cut
    rows = rows.astype(jnp.bfloat16)
    for target in (same, other):
        target[target.shape[0] - 16 :, :] = rows
    for i in range(half):
        mine, theirs = parity * half + i, (1 - parity) * half + i
        own[pl.ds(i * tok, tok), :] = normal(query, q_gain, mine, 0)
        if i < early:
            own[pl.ds((2 * kept - half + i) * tok, tok), :] = normal(key, k_gain, mine, 1)
        else:
            at = pl.ds((i - early) * tok, tok)
            same[at, :] = normal(key, k_gain, mine, 1)
            other[at, :] = normal(key, k_gain, theirs, 1)
    for s in range(2 * half, streams):
        own[pl.ds((s - half) * tok, tok), :] = normal(query, q_gain, s, 0)
        own[pl.ds((kept + s - 2 * half) * tok, tok), :] = normal(key, k_gain, s, 1)


def table_kernel(half, i, block_map, table):
    count = block_map.shape[1]
    s = lax.rem(lax.axis_index("seq"), 2) * half + i if i < half else half + i
    row = lax.broadcasted_iota(jnp.int32, (count, count), 0)
    column = lax.broadcasted_iota(jnp.int32, (count, count), 1)
    table[...] = jnp.zeros_like(table)
    table[:count, :count] = jnp.where((block_map[s] == 1) | (row == column), 0.0, far)


def blocks_of(half, i, bounds, notes):
    n = len(notes)
    tok = notes[0].shape[1]
    padded = bounds.shape[1]
    tail = notes[0].shape[0] % tok
    my_seq = lax.axis_index("seq")
    s = lax.rem(my_seq, 2) * half + i if i < half else half + i
    row_in = lax.broadcasted_iota(jnp.int32, (tok, LANES), 0)
    tokens = [(row_in + lax.bitwise_xor(my_seq, m) * tok).astype(jnp.float32) for m in range(n)]
    low = bounds[pl.ds(2 * s, 1), :]
    high = bounds[pl.ds(2 * s + 1, 1), :]
    blocks = []
    ids = []
    for m in range(n):
        wide = jnp.concatenate([tokens[m]] * (padded // LANES), axis=1)
        blocks.append(one_hot((low <= wide) & (wide < high)))
        rows = notes[m][notes[m].shape[0] - tail :, :].astype(jnp.float32)
        ids.append(rows[2 * i : 2 * i + 1, :] * tok + rows[2 * i + 1 : 2 * i + 2, :])
    hit = jnp.concatenate(
        [jnp.concatenate([one_hot(tokens[m] == ids[j]) for j in range(n)], axis=1) for m in range(n)], axis=0
    )
    return dot(hit, jnp.concatenate(blocks, axis=0), NN).astype(jnp.bfloat16)


def blocks_kernel(half, picks, bounds, *refs):
    tables, refs = refs[: len(picks)], refs[len(picks) :]
    notes, outs = refs[: -2 * len(picks)], refs[-2 * len(picks) :]
    found = [blocks_of(half, i, bounds, notes) for i in picks]
    for at in range(len(picks)):
        outs[2 * at][...] = found[at]
        count = outs[2 * at + 1].shape[0]
        outs[2 * at + 1][...] = dot(found[at][:count], tables[at][...].astype(jnp.bfloat16), NN).astype(jnp.bfloat16)


def mix_all(tasks):
    factor = tasks[0][0].shape[1] ** (-0.5) * math.log2(math.e)
    scores = []
    for normed_q, bias, normed_k, member, _ in tasks:
        scores.append(dot(jnp.concatenate([normed_q, bias], axis=1), jnp.concatenate([normed_k, member], axis=1), NT))
    peaks = [jnp.max(score, axis=1, keepdims=True) for score in scores]
    weights = [jnp.exp2((score - peak) * factor) for score, peak in zip(scores, peaks)]
    denoms = [jnp.sum(weight, axis=1, keepdims=True) for weight in weights]
    mixed = [dot(weight.astype(jnp.bfloat16), task[4], NN) for weight, task in zip(weights, tasks)]
    return [(rows / denom).astype(jnp.bfloat16) for rows, denom in zip(mixed, denoms)]


def peer_kernel(n, half, early, streams, tok, heads, q_gain, k_gain, own, *refs):
    keys, values, refs = refs[:n], refs[n : 2 * n], refs[2 * n :]
    member, bias, (out, normed) = refs[:half], refs[half : 2 * half], refs[2 * half :]
    first_head = lax.rem(lax.axis_index("head") * streams, heads) + lax.rem(lax.axis_index("seq"), 2) * half
    scale_q, *scale_k = columns_of([(keys[1], 0)] + [(keys[m], 1) for m in range(1, n)])
    scale_k = [None] + scale_k
    queries = values[1].shape[0] // tok - half
    tasks = []
    for i in range(half):
        if i < early:
            gain = k_gain[pl.ds(first_head + i, 1), :]
            parts = [own[pl.ds((2 * streams - 3 * half + i) * tok, tok), :]]
            for m in range(1, n):
                raw = values[m][pl.ds((half + i) * tok, tok), :].astype(jnp.float32)
                parts.append((raw * scale_k[m] * gain).astype(jnp.bfloat16))
            normed_k = jnp.concatenate(parts, axis=0)
            normed[i] = normed_k
        else:
            normed_k = jnp.concatenate([keys[m][pl.ds((i - early) * tok, tok), :] for m in range(n)], axis=0)
        value_rows = jnp.concatenate([values[m][pl.ds(i * tok, tok), :] for m in range(n)], axis=0)
        raw = values[1][pl.ds((queries + i) * tok, tok), :].astype(jnp.float32)
        normed_q = (raw * scale_q * q_gain[pl.ds(first_head + i, 1), :]).astype(jnp.bfloat16)
        tasks.append((normed_q, bias[i][tok:], normed_k, member[i][...], value_rows))
    for i, rows in enumerate(mix_all(tasks)):
        out[i] = rows


def columns_of(picks):
    rows = []
    for message, kind in picks:
        tail = message[message.shape[0] - 16 :, :].astype(jnp.float32)
        rows.append((tail[3 * kind : 3 * kind + 1, :] + tail[3 * kind + 1 : 3 * kind + 2, :]) + tail[3 * kind + 2 : 3 * kind + 3, :])
    columns = jnp.concatenate(rows + [rows[0]] * (-len(rows) % 8), axis=0).T
    return [columns[:, at : at + 1] for at in range(len(picks))]


def own_kernel(n, half, early, kept, tok, heads, k_gain, own, normed, *refs):
    keys, values, member, refs = refs[:n], refs[n : 2 * n], refs[2 * n : 2 * n + kept], refs[2 * n + kept :]
    bias, further, out = refs[:kept], refs[kept:-1], refs[-1]
    streams = half + kept
    tasks = []
    first_head = lax.rem(lax.axis_index("head") * streams, heads)
    if kept > half:
        scales = [None] + columns_of([(keys[m], 1) for m in range(1, n)])
    for i in range(kept):
        at = pl.ds(i * tok, tok)
        if i < half:
            parts = [normed[i]] if i < early else [keys[m][pl.ds((i - early) * tok, tok), :] for m in range(n)]
            value_rows = jnp.concatenate([values[m][at, :] for m in range(n)], axis=0)
        else:
            gain = k_gain[pl.ds(first_head + half + i, 1), :]
            parts, value_rows = [own[pl.ds((kept + i - half) * tok, tok), :]], []
            for m in range(n):
                ref, start = further[m], 0
                start = (start + 2 * (i - half)) * tok
                value_rows.append(ref[start : start + tok, :])
                if m:
                    raw = ref[start + tok : start + 2 * tok, :].astype(jnp.float32)
                    parts.append((raw * scales[m] * gain).astype(jnp.bfloat16))
            value_rows = jnp.concatenate(value_rows, axis=0)
        tasks.append((own[at, :], bias[i][:tok], jnp.concatenate(parts, axis=0), member[i][...], value_rows))
    for i, rows in enumerate(mix_all(tasks)):
        out[i] = rows


def local(n, query, key, value, q_gain, k_gain, order, cluster_rows, block_map):
    streams, tok, width = query.shape
    heads = q_gain.shape[0]
    half = streams // 2
    rest = streams - 2 * half
    kept = half + rest
    block_count = block_map.shape[2]
    clusters = cluster_rows.shape[1]
    blocks_per = block_count // clusters
    padded = -(-block_count // LANES) * LANES
    bf16, f32 = jnp.bfloat16, jnp.float32
    head_size = lax.axis_size("head")

    def exchange(rows, m):
        return lax.ppermute(rows, "seq", [(i, i ^ m) for i in range(n)])

    def after(rows, done):
        return lax.optimization_barrier((rows, done))[0]

    tail = -(-2 * kept // 16) * 16
    early = half - half // 2
    lead = half + early
    sized = lambda count: pltpu.VMEM((count * tok + tail, width), bf16)
    note, v_same, v_other, v_plain = pl.pallas_call(
        functools.partial(prep_kernel, half, early, tail),
        out_shape=[pltpu.VMEM((8, tok), f32), sized(lead + 2 * rest), sized(lead + half), sized(lead)],
        in_specs=[ANY] * 4,
        out_specs=[VMEM] * 4,
        scratch_shapes=[
            pltpu.VMEM(query.shape, bf16),
            pltpu.VMEM(key.shape, bf16),
            pltpu.VMEM(order.shape, jnp.int32),
            pltpu.SemaphoreType.DMA((2 * streams + 1 + 3 * lead + 2 * rest + half,)),
        ],
        compiler_params=limit,
    )(*[pltpu.with_memory_space_constraint(x, pltpu.HBM) for x in (query, key, value, order)])

    values, tables = [v_same] + [None] * (n - 1), [None] * kept

    chain = [2**i for i in range(max(heads // streams, 1).bit_length() - 1)]
    launches = [[] for _ in range(len(chain) + 1)]
    fillers = [[] for _ in range(len(chain) + 1)]
    for m in reversed(range(1, n)):
        launches[min(0 if m % 2 == 0 else 1 if m == 1 else 2, len(chain))].append(m)
    for i in range(kept):
        fillers[min(i, len(chain))].append(i)

    def beside(at, note):
        for m in launches[at]:
            message = v_other if m == 1 else v_plain if m % 2 else v_same
            values[m] = exchange(after(message, note) if at else message, m)
        for i in fillers[at]:
            tables[i] = call(
                functools.partial(table_kernel, half, i),
                jax.ShapeDtypeStruct((padded, padded), f32),
                [after(block_map, note)],
                cost=weight,
            )

    beside(0, note)
    for at, step in enumerate(chain):
        note = note + lax.ppermute(note, "head", [(i, i ^ step) for i in range(head_size)])
        beside(at + 1, note)
    rows = lambda count, more: jax.ShapeDtypeStruct((count * tok + more, width), bf16)
    k_same, k_other, own_rows = call(
        functools.partial(norm_kernel, half, early, heads),
        [rows(half - early, 16), rows(half - early, 16), rows(kept + rest + early, 0)],
        [note, query, key, q_gain, k_gain],
        cost=weight,
    )
    keys = [k_same] + [None] * (n - 1)
    for m in reversed(range(1, n)):
        message = k_other if m % 2 else k_same
        keys[m] = exchange(message, m)

    cluster_rows = after(cluster_rows, note)
    start = jnp.cumsum(cluster_rows, axis=1, dtype=jnp.int32) - cluster_rows
    step_rows = jnp.arange(blocks_per, dtype=jnp.int32) * BLOCK
    low = start[:, :, None] + step_rows
    high = jnp.minimum(low + BLOCK, (start + cluster_rows)[:, :, None])
    bounds = jnp.stack([low.reshape(streams, block_count), high.reshape(streams, block_count)], axis=1)
    bounds = jnp.pad(bounds.reshape(2 * streams, block_count).astype(f32), ((0, 0), (0, padded - block_count)))

    member, bias = [None] * kept, [None] * kept
    for picks in [list(range(half)), list(range(half, kept))][: 1 + (rest > 0)]:
        shapes = []
        for i in picks:
            shapes.append(jax.ShapeDtypeStruct((n * tok, padded), bf16))
            shapes.append(jax.ShapeDtypeStruct(((2 if i < half else 1) * tok, padded), bf16))
        made = call(
            functools.partial(blocks_kernel, half, picks),
            shapes,
            [bounds, *[tables[i] for i in picks], *values],
            cost=1000,
        )
        for at, i in enumerate(picks):
            member[i], bias[i] = made[2 * at], made[2 * at + 1]
    across = n // 2
    held = {0: values[0][lead * tok : (lead + 2 * rest) * tok]}
    while rest and across:
        if across == n // 2 and n > 2:
            held[across] = values[across][lead * tok : (lead + 2 * rest) * tok]
        else:
            group = sorted(held)
            sent = jnp.concatenate([held[m] for m in group], axis=0)
            got = exchange(after(sent, member[0]), across)
            size = 2 * rest * tok
            for at, m in enumerate(group):
                held[m ^ across] = got[at * size : (at + 1) * size]
        across //= 2
    further = held if rest else {}

    peer, normed = call(
        functools.partial(peer_kernel, n, half, early, streams, tok, heads),
        [
            jax.ShapeDtypeStruct((half, tok, width), bf16),
            jax.ShapeDtypeStruct((early, n * tok, width), bf16),
        ],
        [q_gain, k_gain, own_rows, *keys, *values, *member[:half], *bias[:half]],
    )
    theirs = exchange(peer, 1)
    own = call(
        functools.partial(own_kernel, n, half, early, kept, tok, heads),
        jax.ShapeDtypeStruct((kept, tok, width), bf16),
        [k_gain, own_rows, normed, *keys, *values, *member, *bias, *[further[m] for m in sorted(further)]],
    )
    even = lax.axis_index("seq") % 2 == 0
    lower = jnp.where(even, own[:half], theirs)
    upper = jnp.where(even, theirs, own[:half])
    return jnp.concatenate([lower, upper, own[half:]], axis=0)


def solution(mesh):
    return jax.shard_map(
        functools.partial(local, mesh.shape["seq"]),
        mesh=mesh,
        in_specs=(
            P("head", "seq", None),
            P("head", "seq", None),
            P("head", "seq", None),
            P(),
            P(),
            P("head", "seq"),
            P("head", None),
            P("head", None, None),
        ),
        out_specs=P("head", "seq", None),
        check_vma=False,
    )
```
